256 devices in a mesh: dp: 32 (over x, z), proto: 8 (over y, core).
Axes of the slice: x: 4, y: 4, z: 8, core: 2. Of those that a mesh axis runs over, the one named last changes fastest.
Arguments:
- student_patches: bfloat16 [16384, 256], P('dp'), may hold values from -16 to 16
- teacher_patches: bfloat16 [16384, 256], P('dp'), may hold values from -16 to 16
- weights_raw: bfloat16 [256, 131072], P(None, 'proto'), may hold values from -2 to 2
- masked_rows: int32 [8192], P('dp'), may hold values from 0 to 511, as said below
Outputs:
- grad_student: float32 [16384, 256], P('dp')
- grad_weight: float32 [256, 131072], P('dp', 'proto')
The draws below stay inside these ranges and needn't reach their ends.
Inputs may be any that keep to these rules, and one draw needn't show every extreme that they name: `masked_rows`: each aligned block of 256 entries names distinct rows of the matching block of 512 patch rows.
All inputs are finite; a program needn't handle non-finite values.
Results may differ from the reference program's by a relative error of at most 0.0032.
Values sent between devices are 32-bit elements; how exact they have to be, the bound alone decides.
A program may use at most 128 MiB of HBM per device.

```python
import jax
import jax.numpy as jnp
from jax import lax

B = 256
PROTO_DEV = 16384
ROWS_DEV = 256
SWEEPS = 3
PATCH_DEV = 512
PROTOS = 131072
PATCHES = 16384
N_DP = 32
N_PROTO = 8


topic_count = 16


def topic_layout(key):
    direction_key, block_key, proto_key = jax.random.split(key, 3)
    topics = jax.random.normal(direction_key, (topic_count, B), jnp.float32)
    block_topic = jax.random.randint(block_key, (N_DP,), 0, topic_count)
    proto_topic = jax.random.randint(proto_key, (PROTOS,), 0, topic_count)
    return (topics, block_topic, proto_topic)


def block_directions(key):
    topics, block_topic, proto_topic = topic_layout(key)
    row_topic = jnp.repeat(block_topic, PATCH_DEV, total_repeat_length=PATCHES)
    return topics[row_topic]


def draw_student_patches(key, part):
    direction = block_directions(key)
    key = jax.random.fold_in(key, 11)
    noise_key, scale_key = jax.random.split(key)
    noise = jax.random.normal(noise_key, (PATCHES, B), jnp.float32)
    along = jnp.exp(jax.random.uniform(scale_key, (PATCHES, 1), jnp.float32, jnp.log(0.2), jnp.log(1.5)))
    return jnp.clip(noise + along * direction, -16.0, 16.0).astype(jnp.bfloat16)


def draw_teacher_patches(key, part):
    direction = block_directions(key)
    key = jax.random.fold_in(key, 12)
    noise_key, scale_key = jax.random.split(key)
    noise = jax.random.normal(noise_key, (PATCHES, B), jnp.float32)
    along = jnp.exp(jax.random.uniform(scale_key, (PATCHES, 1), jnp.float32, jnp.log(0.2), jnp.log(1.5)))
    return jnp.clip(noise + along * direction, -16.0, 16.0).astype(jnp.bfloat16)


def draw_weights_raw(key, part):
    topics, block_topic, proto_topic = topic_layout(key)
    key = jax.random.fold_in(key, 13)
    noise_key, lean_key = jax.random.split(key)
    noise = jax.random.normal(noise_key, (B, PROTOS), jnp.float32)
    lean = jax.random.uniform(lean_key, (1, PROTOS), jnp.float32, 0.2, 1.5)
    direction = topics.T[:, proto_topic]
    values = (noise + lean * direction) * B ** (-0.5)
    return jnp.clip(values, -2.0, 2.0).astype(jnp.bfloat16)


def draw_masked_rows(key, part):
    key = jax.random.fold_in(key, 14)
    block_keys = jax.random.split(key, N_DP)
    chosen = jax.vmap(lambda block_key: jax.random.permutation(block_key, PATCH_DEV)[:ROWS_DEV])(block_keys)
    return chosen.reshape(N_DP * ROWS_DEV).astype(jnp.int32)


def setup_inputs(seed: int = 0) -> dict:
    key_of = jax.random.split(jax.random.key(seed), 5)
    student_patches = draw_student_patches(jax.random.fold_in(key_of[4], 71), 0)
    teacher_patches = draw_teacher_patches(jax.random.fold_in(key_of[4], 71), 0)
    weights_raw = draw_weights_raw(jax.random.fold_in(key_of[4], 71), 0)
    masked_rows = draw_masked_rows(jax.random.fold_in(key_of[4], 71), 0)
    return {"student_patches": student_patches, "teacher_patches": teacher_patches, "weights_raw": weights_raw, "masked_rows": masked_rows}


teacher_temp = 0.07
student_temp = 0.1
loss_scale = 2048.0

def unit_rows(values):
    norm_value = jnp.sqrt(lax.optimization_barrier(jnp.sum(values * values, axis=-1, keepdims=True)) + 1e-06)
    return (values / norm_value, norm_value)

def reference(student_patches, teacher_patches, weights_raw, masked_rows):
    block_start = (jnp.arange(N_DP * ROWS_DEV) // ROWS_DEV * PATCH_DEV).astype(jnp.int32)
    picked_rows = block_start + masked_rows.astype(jnp.int32)
    student_unit, student_norm = unit_rows(student_patches[picked_rows].astype(jnp.float32))
    teacher_unit, teacher_norm = unit_rows(teacher_patches[picked_rows].astype(jnp.float32))
    student_half = student_unit.astype(jnp.bfloat16)
    teacher_half = teacher_unit.astype(jnp.bfloat16)
    weights = weights_raw.astype(jnp.float32)
    weight_norm = jnp.sqrt(lax.optimization_barrier(jnp.sum(weights * weights, axis=0)) + 1e-06)
    proto_unit = weights / weight_norm
    proto_half = proto_unit.astype(jnp.bfloat16)
    proto_blocks = proto_half.reshape(B, N_PROTO, PROTO_DEV).transpose(1, 0, 2)

    def teacher_block(block):
        return jnp.exp(jnp.dot(teacher_half, block, preferred_element_type=jnp.float32) / teacher_temp).astype(jnp.bfloat16)
    teacher_table = lax.map(teacher_block, proto_blocks)
    row_scale = jnp.ones((N_DP * ROWS_DEV,), jnp.float32)
    col_scale = jnp.ones((N_PROTO, PROTO_DEV), jnp.float32)
    for sweep_index in range(SWEEPS):
        current_rows = row_scale
        col_total = lax.map(lambda entry: lax.optimization_barrier(jnp.sum(current_rows[:, None] * entry.astype(jnp.float32), axis=0)), teacher_table)
        col_scale = 1.0 / col_total
        row_parts = lax.map(lambda pair: lax.optimization_barrier(jnp.sum(pair[0].astype(jnp.float32) * pair[1][None, :], axis=1)), (teacher_table, col_scale))
        row_scale = 1.0 / lax.optimization_barrier(jnp.sum(row_parts, axis=0))

    def student_block(block):
        scores = jnp.dot(student_half, block, preferred_element_type=jnp.float32) / student_temp
        return lax.optimization_barrier(jnp.sum(jnp.exp(scores), axis=1))
    student_total = lax.optimization_barrier(jnp.sum(lax.map(student_block, proto_blocks), axis=0))

    def backward_block(carry, inputs):
        block, entry, col_part = inputs
        scores = jnp.dot(student_half, block, preferred_element_type=jnp.float32) / student_temp
        probs = jnp.exp(scores) / student_total[:, None]
        target = entry.astype(jnp.float32) * row_scale[:, None] * col_part[None, :]
        dscore = (loss_scale / student_temp * (probs - target)).astype(jnp.bfloat16)
        unit_part = jnp.dot(dscore, block.T, preferred_element_type=jnp.float32)
        grad_block = jnp.dot(student_half.T, dscore, preferred_element_type=jnp.float32)
        return (carry + unit_part, grad_block)
    unit_grad, grad_blocks = lax.scan(backward_block, jnp.zeros((N_DP * ROWS_DEV, B), jnp.float32), (proto_blocks, teacher_table, col_scale))
    proto_grad = grad_blocks.transpose(1, 0, 2).reshape(B, N_PROTO * PROTO_DEV)
    column_dot = lax.optimization_barrier(jnp.sum(proto_unit * proto_grad, axis=0))
    grad_weight = (proto_grad - proto_unit * column_dot[None, :]) / weight_norm[None, :]
    row_grad = (unit_grad - student_unit * lax.optimization_barrier(jnp.sum(student_unit * unit_grad, axis=1, keepdims=True))) / student_norm
    grad_student = jnp.zeros((N_DP * PATCH_DEV, B), jnp.float32).at[picked_rows].set(row_grad)
    return (grad_student, grad_weight)
```

```python
import functools
import math

import jax
import jax.numpy as jnp
from jax import lax
from jax.experimental import pallas as pl
from jax.experimental.pallas import tpu as pltpu
from jax.sharding import PartitionSpec as P

MESH = pl.DeviceIdType.MESH
F32 = jnp.float32
BF16 = jnp.bfloat16
SWEEPS = 3
TEACHER_TEMP = 0.07
STUDENT_TEMP = 0.1
LOSS_SCALE = 2048.0
LOG2E = math.log2(math.e)
LANES = 128
TILES = 8
STREAMS = 4


class Sizes:
    def __init__(self, mesh_shape, width, patches, rows, protos):
        n_dp, n_proto = mesh_shape
        self.nc = 2
        self.ny = n_proto // 2
        self.nx = 4 if n_dp >= 16 else 2
        self.nz = n_dp // self.nx
        self.width = width
        self.patches = patches
        self.rows = rows
        self.all_rows = rows * self.nx
        self.cols_dp = protos
        self.cols = protos // self.nx
        self.tile = self.cols // TILES
        self.sub = self.cols // STREAMS
        self.bw = width // n_dp
        self.group = self.nx * self.ny * self.nc
        self.packed = self.all_rows // LANES
        self.share = rows // (self.ny * self.nc)
        self.steps = self.nz - 1


def bulk_wait(ref, sem):
    pltpu.make_async_copy(ref, ref, sem).wait()


def kernel(
    sz, mask_ref, stu_ref, tea_ref, w_hbm, gs_ref, gw_ref,
    wbuf, ph, winv, tbuf, sbuf, snorm, sht, table, expo,
    colacc, colv, colmsg, colbuf, racc, sacc, rscale, sscale,
    rmsg0, rmsg1, rmsg2, rbuf0, rbuf1, rbuf2,
    dbuf, unit, ubuf, ugrad, grad, ring, rowg,
    w_sem, ts_send, ts_recv, fw_send, fw_recv, col_send, col_recv, row_send, row_recv,
    u_send, u_recv, g_send, g_recv, ring_send, ring_recv, x_send, x_recv,
):
    nx, ny, nc, nz = sz.nx, sz.ny, sz.nc, sz.nz
    rows, cols, tile, sub = sz.rows, sz.cols, sz.tile, sz.sub
    chunks = tile // LANES
    rmsg = (rmsg0, rmsg1, rmsg2)
    rbuf = (rbuf0, rbuf1, rbuf2)
    dp = lax.axis_index("dp")
    pr = lax.axis_index("proto")
    x, z = dp // nz, dp % nz
    y, c = pr // nc, pr % nc
    half = rows // nc

    def place(xx, zz, yy, cc):
        return (xx * nz + zz, yy * nc + cc)

    def group_peer(k):
        xx = (x + k // (ny * nc)) % nx
        yy = (y + (k // nc) % ny) % ny
        cc = (c + k % nc) % nc
        return xx, yy, cc

    def proto_peer(k):
        yy = (y + k // nc) % ny
        cc = (c + k % nc) % nc
        return yy, cc

    w_copy = pltpu.make_async_copy(
        w_hbm.at[:, pl.ds(pl.multiple_of(x * cols, cols), cols)], wbuf, w_sem
    )
    w_copy.start()

    barrier = pltpu.get_barrier_semaphore()

    @pl.loop(1, sz.group)
    def _(k):
        xx, yy, cc = group_peer(k)
        pl.semaphore_signal(barrier, inc=1, device_id=place(xx, z, yy, cc), device_id_type=MESH)

    @pl.loop(1, nz)
    def _(k):
        pl.semaphore_signal(
            barrier, inc=1, device_id=place(x, (z + k) % nz, y, c), device_id_type=MESH
        )

    def one_hot_t():
        at = lax.broadcasted_iota(jnp.int32, (sz.patches, rows), 0)
        return jnp.where(at == mask_ref[...], 1.0, 0.0).astype(BF16)

    def unit_rows(ref):
        picked = lax.dot_general(
            one_hot_t(), ref[...], (((0,), (0,)), ((), ())), preferred_element_type=F32
        )
        norm = jnp.sqrt(jnp.sum(picked * picked, axis=1, keepdims=True) + 1e-06)
        return picked / norm, norm

    tea_unit, _ = unit_rows(tea_ref)
    tbuf[x] = tea_unit
    stu_unit, stu_norm = unit_rows(stu_ref)
    sbuf[x] = stu_unit
    snorm[...] = jnp.broadcast_to(stu_norm, (rows, LANES))

    pl.semaphore_wait(barrier, sz.group - 1 + nz - 1)

    def spread(buf, which, d):
        return pltpu.make_async_remote_copy(
            src_ref=buf.at[x, pl.ds(pl.multiple_of(c * half, half), half)],
            dst_ref=buf.at[x, pl.ds(pl.multiple_of(c * half, half), half)],
            send_sem=ts_send.at[which, d - 1],
            recv_sem=ts_recv.at[which, d - 1],
            device_id=place((x + d) % nx, z, y, c),
            device_id_type=MESH,
        )

    def forward(buf, which, d):
        part = buf.at[(x + nx - d) % nx, pl.ds(pl.multiple_of(c * half, half), half)]
        return pltpu.make_async_remote_copy(
            src_ref=part,
            dst_ref=part,
            send_sem=fw_send.at[which, d - 1],
            recv_sem=fw_recv.at[which, d - 1],
            device_id=place(x, z, y, 1 - c),
            device_id_type=MESH,
        )

    for which, buf in ((0, tbuf), (1, sbuf)):
        for d in range(1, nx):
            spread(buf, which, d).start()

    w_copy.wait()

    @pl.loop(0, TILES)
    def _(t):
        at = pl.ds(pl.multiple_of(t * tile, tile), tile)
        w = wbuf[:, at].astype(F32)
        inv = 1.0 / jnp.sqrt(jnp.sum(w * w, axis=0, keepdims=True) + 1e-06)
        winv[:, at] = inv
        ph[:, at] = (w * inv).astype(BF16)
        colacc[:, at] = jnp.zeros((1, tile), F32)

    def teacher_block(xb):
        half_rows = tbuf[xb].astype(BF16)
        at_rows = pl.ds(pl.multiple_of(xb * rows, rows), rows)

        @pl.loop(0, TILES)
        def _(t):
            at = pl.ds(pl.multiple_of(t * tile, tile), tile)
            dots = jnp.dot(half_rows, ph[:, at], preferred_element_type=F32)
            entry = jnp.exp2(dots * (LOG2E / TEACHER_TEMP)).astype(BF16)
            table[at_rows, at] = entry
            colacc[:, at] += jnp.sum(entry.astype(F32), axis=0, keepdims=True)

    def student_block(xb):
        half_rows = sbuf[xb].astype(BF16)
        at_rows = pl.ds(pl.multiple_of(xb * rows, rows), rows)
        sht[:, at_rows] = jnp.transpose(sbuf[xb]).astype(BF16)
        sacc[at_rows, :] = jnp.zeros((rows, LANES), F32)

        @pl.loop(0, TILES)
        def _(t):
            at = pl.ds(pl.multiple_of(t * tile, tile), tile)
            dots = jnp.dot(half_rows, ph[:, at], preferred_element_type=F32)
            ex = jnp.exp2(dots * (LOG2E / STUDENT_TEMP))
            expo[at_rows, at] = ex
            total = ex[:, 0:LANES]
            for i in range(1, chunks):
                total = total + ex[:, i * LANES:(i + 1) * LANES]
            sacc[at_rows, :] += total

    teacher_block(x)
    student_block(x)
    for d in range(1, nx):
        spread(tbuf, 0, d).wait_recv()
        forward(tbuf, 0, d).start()
    for d in range(1, nx):
        pltpu.make_async_copy(
            tbuf.at[0, pl.ds(0, half)], tbuf.at[0, pl.ds(0, half)], fw_recv.at[0, d - 1]
        ).wait()
        teacher_block((x + nx - d) % nx)
    for d in range(1, nx):
        spread(sbuf, 1, d).wait_recv()
        forward(sbuf, 1, d).start()

    def student_arrived(d):
        pltpu.make_async_copy(
            sbuf.at[0, pl.ds(0, half)], sbuf.at[0, pl.ds(0, half)], fw_recv.at[1, d - 1]
        ).wait()
        student_block((x + nx - d) % nx)

    def pack(ref):
        parts = []
        for i in range(sz.packed):
            block = ref[i * LANES:(i + 1) * LANES, :]
            parts.append(jnp.sum(jnp.transpose(block), axis=0, keepdims=True))
        return jnp.concatenate(parts, axis=0)

    def unpack(value, ref):
        for i in range(sz.packed):
            block = jnp.broadcast_to(value[i:i + 1, :], (LANES, LANES))
            ref[i * LANES:(i + 1) * LANES, :] = jnp.transpose(block)

    def col_exchange_start(sweep):
        colmsg[sweep] = colacc[...]

        @pl.loop(1, nz)
        def _(k):
            pltpu.make_async_remote_copy(
                src_ref=colmsg.at[sweep],
                dst_ref=colbuf.at[sweep, k - 1],
                send_sem=col_send.at[sweep],
                recv_sem=col_recv.at[sweep],
                device_id=place(x, (z + k) % nz, y, c),
                device_id_type=MESH,
            ).start()

    def col_exchange_end(sweep):
        bulk_wait(colbuf.at[sweep], col_recv.at[sweep])
        total = colacc[...]
        for k in range(nz - 1):
            total = total + colbuf[sweep, k]
        colv[...] = 1.0 / total

    def row_pass():
        @pl.loop(0, nx)
        def _(i):
            at_rows = pl.ds(pl.multiple_of(i * rows, rows), rows)

            def step(t, acc):
                for j in range(chunks):
                    at = pl.ds(pl.multiple_of(t * tile + j * LANES, LANES), LANES)
                    acc = acc + table[at_rows, at].astype(F32) * colv[:, at]
                return acc

            racc[at_rows, :] = lax.fori_loop(0, TILES, step, jnp.zeros((rows, LANES), F32))

    def col_pass():
        @pl.loop(0, TILES)
        def _(t):
            for j in range(chunks):
                at = pl.ds(pl.multiple_of(t * tile + j * LANES, LANES), LANES)
                weighted = table[:, at].astype(F32) * rscale[...]
                colacc[:, at] = jnp.sum(weighted, axis=0, keepdims=True)

    def row_exchange_start(sweep):
        @pl.loop(1, sz.group)
        def _(k):
            xx, yy, cc = group_peer(k)
            pltpu.make_async_remote_copy(
                src_ref=rmsg[sweep],
                dst_ref=rbuf[sweep].at[k - 1],
                send_sem=row_send.at[sweep],
                recv_sem=row_recv.at[sweep],
                device_id=place(xx, z, yy, cc),
                device_id_type=MESH,
            ).start()

    def row_exchange_end(sweep):
        bulk_wait(rbuf[sweep], row_recv.at[sweep])
        return rmsg[sweep][...] + jnp.sum(rbuf[sweep][...], axis=0)

    for sweep in range(SWEEPS):
        if sweep > 0:
            col_pass()
        col_exchange_start(sweep)
        if sweep == 0:
            for d in range(1, (nx + 1) // 2 + 1):
                student_arrived(d)
        col_exchange_end(sweep)
        row_pass()
        rmsg[sweep][0:sz.packed, :] = pack(racc)
        if sweep == 1:
            rmsg[sweep][sz.packed:, :] = pack(sacc)
        row_exchange_start(sweep)
        if sweep == 0:
            for d in range((nx + 1) // 2 + 1, nx):
                student_arrived(d)
        total = row_exchange_end(sweep)
        if sweep == 1:
            unpack((LOSS_SCALE / STUDENT_TEMP) / total[sz.packed:, :], sscale)
            total = total[0:sz.packed, :]
        if sweep == SWEEPS - 1:
            unpack((LOSS_SCALE / STUDENT_TEMP) / total, rscale)
        else:
            unpack(1.0 / total, rscale)

    unit[...] = jnp.zeros(unit.shape, F32)

    def gradient_tile(t):
        at = pl.ds(pl.multiple_of(t * tile, tile), tile)
        proto = ph[:, at]

        @pl.loop(0, nx)
        def _(i):
            at_rows = pl.ds(pl.multiple_of(i * rows, rows), rows)
            by_row = sscale[at_rows, :]
            by_row_t = rscale[at_rows, :]
            for j in range(chunks):
                at_j = pl.ds(pl.multiple_of(t * tile + j * LANES, LANES), LANES)
                target = (table[at_rows, at_j].astype(F32) * by_row_t) * colv[:, at_j]
                score = expo[at_rows, at_j] * by_row - target
                dbuf[at_rows, j * LANES:(j + 1) * LANES] = score.astype(BF16)
            unit[at_rows, :] += lax.dot_general(
                dbuf[at_rows, :], proto, (((1,), (1,)), ((), ())), preferred_element_type=F32
            )

        pg = jnp.dot(sht[...], dbuf[...], preferred_element_type=F32)
        inv = winv[:, at]
        pu = wbuf[:, at].astype(F32) * inv
        dots = jnp.sum(pu * pg, axis=0, keepdims=True)
        out = (pg - pu * dots) * inv
        grad[:, :, :, at] = out.reshape(nx, nz, sz.bw, tile)

    def ring_block(stream, s):
        if stream // 2 == 0:
            return (z + 2 * nz - 1 - s) % nz
        return (z + 1 + s) % nz

    def ring_peer(stream):
        step = 1 if stream // 2 == 0 else nz - 1
        return place(x, (z + step) % nz, y, c)

    def ring_send_copy(stream, s, src):
        return pltpu.make_async_remote_copy(
            src_ref=src,
            dst_ref=ring.at[stream, s],
            send_sem=ring_send.at[stream, s],
            recv_sem=ring_recv.at[stream, s],
            device_id=ring_peer(stream),
            device_id_type=MESH,
        )

    def stream_at(stream):
        return pl.ds(stream * sub, sub)

    def begin(stream):
        block = grad.at[:, ring_block(stream, 0), :, stream_at(stream)]
        ring_send_copy(stream, 0, block).start()

    def serve(stream, s, last=False):
        slot = ring.at[stream, s]
        bulk_wait(slot, ring_recv.at[stream, s])
        slot[...] = slot[...] + grad[:, ring_block(stream, s + 1), :, stream_at(stream)]
        if not last:
            ring_send_copy(stream, s + 1, slot).start()

    def deliver(stream):
        out_at = pl.ds(pl.multiple_of(x * cols + stream * sub, sub), sub)
        for d in range(1, nx):
            xx = (x + d) % nx
            pltpu.make_async_remote_copy(
                src_ref=ring.at[stream, sz.steps - 1, xx],
                dst_ref=gw_ref.at[:, out_at],
                send_sem=x_send.at[stream, d - 1],
                recv_sem=x_recv.at[stream, d - 1],
                device_id=place(xx, z, y, c),
                device_id_type=MESH,
            ).start()
        gw_ref[:, out_at] = ring[stream, sz.steps - 1, x]

    per_stream = TILES // STREAMS
    order = (0, 2, 1, 3)
    for n, stream in enumerate(order):
        @pl.loop(0, per_stream)
        def _(i):
            gradient_tile(stream * per_stream + i)

        begin(stream)
        if n == 2:
            serve(order[0], 0, last=sz.steps == 1)

    @pl.loop(1, sz.group)
    def _(k):
        xx, yy, cc = group_peer(k)
        first = xx * rows + (yy * nc + cc) * sz.share
        pltpu.make_async_remote_copy(
            src_ref=unit.at[pl.ds(pl.multiple_of(first, sz.share), sz.share)],
            dst_ref=ubuf.at[k - 1],
            send_sem=u_send,
            recv_sem=u_recv,
            device_id=place(xx, z, yy, cc),
            device_id_type=MESH,
        ).start()

    def ring_steps(first, last):
        @pl.loop(first, last)
        def _(s):
            for stream in order[1:]:
                serve(stream, s)
            serve(order[0], s + 1)

    middle = (sz.steps - 2) // 2
    if sz.steps >= 3:
        ring_steps(0, middle)

    mine = pl.ds(pl.multiple_of((y * nc + c) * sz.share, sz.share), sz.share)
    bulk_wait(ubuf, u_recv)
    first = pl.multiple_of(x * rows + (y * nc + c) * sz.share, sz.share)
    total = unit[pl.ds(first, sz.share), :]
    for k in range(sz.group - 1):
        total = total + ubuf[k]
    unit_mine = sbuf[x, mine]
    along = jnp.sum(unit_mine * total, axis=1, keepdims=True)
    rowg[mine, :] = (total - unit_mine * along) / snorm[mine, 0:1]

    @pl.loop(1, ny * nc)
    def _(k):
        yy, cc = proto_peer(k)
        pltpu.make_async_remote_copy(
            src_ref=rowg.at[mine],
            dst_ref=rowg.at[mine],
            send_sem=g_send,
            recv_sem=g_recv,
            device_id=place(x, z, yy, cc),
            device_id_type=MESH,
        ).start()

    if sz.steps >= 2:
        ring_steps(max(middle, 0), sz.steps - 2)
        for stream in order[1:]:
            serve(stream, sz.steps - 2)
        serve(order[0], sz.steps - 1, last=True)
    deliver(order[0])
    for stream in order[1:]:
        serve(stream, sz.steps - 1, last=True)
        deliver(stream)

    others = pl.ds(0, rows - sz.share)
    bulk_wait(rowg.at[others], g_recv)
    bulk_wait(rowg.at[others], g_send)
    picks = one_hot_t()
    rest = rowg[...]
    out = None
    for _ in range(3):
        part = rest.astype(BF16)
        rest = rest - part.astype(F32)
        term = jnp.dot(picks, part, preferred_element_type=F32)
        out = term if out is None else out + term
    gs_ref[...] = out

    for which, buf in ((0, tbuf), (1, sbuf)):
        for d in range(1, nx):
            spread(buf, which, d).wait_send()
            forward(buf, which, d).wait_send()
    for sweep in range(SWEEPS):
        bulk_wait(colbuf.at[sweep], col_send.at[sweep])
        bulk_wait(rbuf[sweep], row_send.at[sweep])
    bulk_wait(ubuf, u_send)
    for stream in range(STREAMS):
        @pl.loop(0, sz.steps)
        def _(s):
            bulk_wait(ring.at[stream, s], ring_send.at[stream, s])

        for d in range(1, nx):
            bulk_wait(ring.at[stream, 0, 0], x_send.at[stream, d - 1])
            bulk_wait(ring.at[stream, 0, 0], x_recv.at[stream, d - 1])


def per_device(sz, student_patches, teacher_patches, weights_raw, masked_rows):
    vmem = pl.BlockSpec(memory_space=pltpu.VMEM)
    dma = pltpu.SemaphoreType.DMA
    g = sz.group
    nx, nz = sz.nx, sz.nz
    p = sz.packed
    scratch = [
        pltpu.VMEM((sz.width, sz.cols), BF16),
        pltpu.VMEM((sz.width, sz.cols), BF16),
        pltpu.VMEM((1, sz.cols), F32),
        pltpu.VMEM((nx, sz.rows, sz.width), F32),
        pltpu.VMEM((nx, sz.rows, sz.width), F32),
        pltpu.VMEM((sz.rows, LANES), F32),
        pltpu.VMEM((sz.width, sz.all_rows), BF16),
        pltpu.VMEM((sz.all_rows, sz.cols), BF16),
        pltpu.VMEM((sz.all_rows, sz.cols), F32),
        pltpu.VMEM((1, sz.cols), F32),
        pltpu.VMEM((1, sz.cols), F32),
        pltpu.VMEM((SWEEPS, 1, sz.cols), F32),
        pltpu.VMEM((SWEEPS, nz - 1, 1, sz.cols), F32),
        pltpu.VMEM((sz.all_rows, LANES), F32),
        pltpu.VMEM((sz.all_rows, LANES), F32),
        pltpu.VMEM((sz.all_rows, LANES), F32),
        pltpu.VMEM((sz.all_rows, LANES), F32),
        pltpu.VMEM((p, LANES), F32),
        pltpu.VMEM((2 * p, LANES), F32),
        pltpu.VMEM((p, LANES), F32),
        pltpu.VMEM((g - 1, p, LANES), F32),
        pltpu.VMEM((g - 1, 2 * p, LANES), F32),
        pltpu.VMEM((g - 1, p, LANES), F32),
        pltpu.VMEM((sz.all_rows, sz.tile), BF16),
        pltpu.VMEM((sz.all_rows, sz.width), F32),
        pltpu.VMEM((g - 1, sz.share, sz.width), F32),
        pltpu.VMEM((sz.share, sz.width), F32),
        pltpu.VMEM((nx, nz, sz.bw, sz.cols), F32),
        pltpu.VMEM((STREAMS, sz.steps, nx, sz.bw, sz.sub), F32),
        pltpu.VMEM((sz.rows, sz.width), F32),
        dma(()),
        dma((2, nx - 1)),
        dma((2, nx - 1)),
        dma((2, nx - 1)),
        dma((2, nx - 1)),
        dma((SWEEPS,)),
        dma((SWEEPS,)),
        dma((SWEEPS,)),
        dma((SWEEPS,)),
        dma(()),
        dma(()),
        dma(()),
        dma(()),
        dma((STREAMS, sz.steps)),
        dma((STREAMS, sz.steps)),
        dma((STREAMS, nx - 1)),
        dma((STREAMS, nx - 1)),
    ]
    return pl.pallas_call(
        functools.partial(kernel, sz),
        out_shape=(
            jax.ShapeDtypeStruct((sz.patches, sz.width), F32),
            jax.ShapeDtypeStruct((sz.bw, sz.cols_dp), F32),
        ),
        in_specs=[vmem, vmem, vmem, pl.BlockSpec(memory_space=pl.ANY)],
        out_specs=(vmem, vmem),
        scratch_shapes=scratch,
        compiler_params=pltpu.CompilerParams(
            collective_id=0, has_side_effects=True, vmem_limit_bytes=56 * 1024 * 1024
        ),
        cost_estimate=pl.CostEstimate(
            flops=8 * sz.all_rows * sz.cols * sz.width,
            bytes_accessed=4 * sz.width * sz.cols,
            transcendentals=2 * sz.all_rows * sz.cols,
        ),
    )(masked_rows.reshape(1, sz.rows), student_patches, teacher_patches, weights_raw)


def solution(mesh):
    placed = (P("dp", None), P("dp", None), P(None, "proto"), P("dp"))
    mesh_shape = (mesh.shape["dp"], mesh.shape["proto"])

    def body(student_patches, teacher_patches, weights_raw, masked_rows):
        sz = Sizes(
            mesh_shape,
            weights_raw.shape[0],
            student_patches.shape[0],
            masked_rows.shape[0],
            weights_raw.shape[1],
        )
        return per_device(sz, student_patches, teacher_patches, weights_raw, masked_rows)

    return jax.shard_map(
        body,
        mesh=mesh,
        in_specs=placed,
        out_specs=(P("dp", None), P("dp", "proto")),
        check_vma=False,
    )
```

```python
import functools
import math

import jax
import jax.numpy as jnp
from jax import lax
from jax.experimental import pallas as pl
from jax.experimental.pallas import tpu as pltpu
from jax.sharding import PartitionSpec as P

MESH = pl.DeviceIdType.MESH
F32 = jnp.float32
BF16 = jnp.bfloat16
SWEEPS = 3
TEACHER_TEMP = 0.07
STUDENT_TEMP = 0.1
LOSS_SCALE = 2048.0
LOG2E = math.log2(math.e)
LANES = 128
TILES = 8
PARTS = 4
BLOCK = 128


class Sizes:
    def __init__(self, mesh_shape, width, patches, rows, protos):
        n_dp, n_proto = mesh_shape
        self.nc = 2
        self.ny = n_proto // 2
        self.nx = 4 if n_dp >= 16 else 2
        self.nz = n_dp // self.nx
        self.width = width
        self.patches = patches
        self.rows = rows
        self.all_rows = rows * self.nx
        self.cols_dp = protos
        self.cols = protos // self.nx
        self.tile = self.cols // TILES
        self.part = self.cols // PARTS
        self.bw = width // n_dp
        self.group = self.nx * self.ny * self.nc
        self.packed = self.all_rows // LANES
        self.share = rows // (self.ny * self.nc)
        self.steps = self.nz - 1


def bulk_wait(ref, sem):
    pltpu.make_async_copy(ref, ref, sem).wait()


def ring_distance(step, size):
    return min(step, size - step)


def kernel(
    sz, mask_ref, stu_hbm, tea_hbm, w_hbm, rowg, gw_ref,
    stu_ref, tea_ref, wbuf, ph, pht, winv, tbuf, sbuf, snorm, sht, table, expo,
    acc8, colv, colmsg, colbuf, racc, sacc, rscale, sscale,
    rmsg0, rmsg1, rmsg2, rbuf0, rbuf1, rbuf2,
    dbuf, unit, ubuf, grad, ring,
    in_sem, w_sem, own_sem, ts_send, ts_recv, fw_send, fw_recv, col_send, col_recv,
    row_send, row_recv, u_send, u_recv, g_send, g_recv, ring_send, ring_recv, x_send, x_recv,
):
    nx, ny, nc, nz = sz.nx, sz.ny, sz.nc, sz.nz
    rows, cols, tile, part = sz.rows, sz.cols, sz.tile, sz.part
    chunks = tile // LANES
    blocks = sz.all_rows // BLOCK
    rmsg = (rmsg0, rmsg1, rmsg2)
    rbuf = (rbuf0, rbuf1, rbuf2)
    dp = lax.axis_index("dp")
    pr = lax.axis_index("proto")
    x, z = dp // nz, dp % nz
    y, c = pr // nc, pr % nc
    half = rows // nc

    xs = [x] + [(x + d) % nx for d in range(1, nx)]
    ys = [y] + [(y + d) % ny for d in range(1, ny)]
    cs = [c] + [(c + d) % nc for d in range(1, nc)]
    zs = [z] + [(z + d) % nz for d in range(1, nz)]

    def place(xx, zz, yy, cc):
        return (xx * nz + zz, yy * nc + cc)

    group = []
    for k in range(1, sz.group):
        dx, dy, dc = k // (ny * nc), (k // nc) % ny, k % nc
        far = ring_distance(dx, nx) + ring_distance(dy, ny)
        group.append((-far, k, xs[dx], ys[dy], cs[dc]))
    group.sort(key=lambda entry: entry[:2])
    z_order = sorted(range(1, nz), key=lambda d: -ring_distance(d, nz))

    barrier = pltpu.get_barrier_semaphore()
    for _, _, xx, yy, cc in group:
        pl.semaphore_signal(barrier, inc=1, device_id=place(xx, z, yy, cc), device_id_type=MESH)
    for d in z_order:
        pl.semaphore_signal(barrier, inc=1, device_id=place(x, zs[d], y, c), device_id_type=MESH)

    tea_copy = pltpu.make_async_copy(tea_hbm, tea_ref, in_sem.at[0])
    stu_copy = pltpu.make_async_copy(stu_hbm, stu_ref, in_sem.at[1])
    w_copy = pltpu.make_async_copy(
        w_hbm.at[:, pl.ds(pl.multiple_of(x * cols, cols), cols)], wbuf, w_sem
    )
    tea_copy.start()
    stu_copy.start()
    w_copy.start()

    at = lax.broadcasted_iota(jnp.int32, (sz.patches, rows), 0)
    one_hot_t = jnp.where(at == mask_ref[...], 1.0, 0.0).astype(BF16)

    def unit_rows(ref):
        picked = lax.dot_general(
            one_hot_t, ref[...], (((0,), (0,)), ((), ())), preferred_element_type=F32
        )
        norm = jnp.sqrt(jnp.sum(picked * picked, axis=1, keepdims=True) + 1e-06)
        return picked / norm, norm

    tea_copy.wait()
    tbuf[x] = unit_rows(tea_ref)[0]
    stu_copy.wait()
    stu_unit, stu_norm = unit_rows(stu_ref)
    sbuf[x] = stu_unit
    snorm[...] = jnp.broadcast_to(stu_norm, (rows, LANES))

    pl.semaphore_wait(barrier, sz.group - 1 + nz - 1)

    my_half = pl.ds(pl.multiple_of(c * half, half), half)

    def spread(buf, which, d):
        return pltpu.make_async_remote_copy(
            src_ref=buf.at[x, my_half],
            dst_ref=buf.at[x, my_half],
            send_sem=ts_send.at[which, d - 1],
            recv_sem=ts_recv.at[which, d - 1],
            device_id=place(xs[d], z, y, c),
            device_id_type=MESH,
        )

    def forward(buf, which, d):
        return pltpu.make_async_remote_copy(
            src_ref=buf.at[xs[nx - d], my_half],
            dst_ref=buf.at[xs[nx - d], my_half],
            send_sem=fw_send.at[which, d - 1],
            recv_sem=fw_recv.at[which, d - 1],
            device_id=place(x, z, y, cs[1]),
            device_id_type=MESH,
        )

    x_order = sorted(range(1, nx), key=lambda d: ring_distance(d, nx))
    for d in x_order:
        spread(tbuf, 0, d).start()

    w_copy.wait()
    for t in range(TILES):
        at = pl.ds(t * tile, tile)
        w = wbuf[:, at].astype(F32)
        inv = 1.0 / jnp.sqrt(jnp.sum(w * w, axis=0, keepdims=True) + 1e-06)
        winv[:, at] = inv
        proto = (w * inv).astype(BF16)
        ph[:, at] = proto
        pht[at, :] = jnp.transpose(proto)

    def col_send_part(sweep, q):
        at = pl.ds(q * part, part)
        colmsg[sweep, q] = jnp.sum(acc8[:, at], axis=0, keepdims=True)
        for d in z_order:
            pltpu.make_async_remote_copy(
                src_ref=colmsg.at[sweep, q],
                dst_ref=colbuf.at[sweep, q, d - 1],
                send_sem=col_send.at[sweep, q],
                recv_sem=col_recv.at[sweep, q],
                device_id=place(x, zs[d], y, c),
                device_id_type=MESH,
            ).start()

    def col_recv_part(sweep, q):
        bulk_wait(colbuf.at[sweep, q], col_recv.at[sweep, q])
        total = colmsg[sweep, q]
        for k in range(nz - 1):
            total = total + colbuf[sweep, q, k]
        colv[:, pl.ds(q * part, part)] = 1.0 / total

    def teacher_block(xb, first=False, last=False):
        half_rows = tbuf[xb].astype(BF16)
        at_rows = pl.ds(pl.multiple_of(xb * rows, rows), rows)
        for t in range(TILES):
            at = pl.ds(t * tile, tile)
            dots = jnp.dot(half_rows, ph[:, at], preferred_element_type=F32)
            entry = jnp.exp2(dots * (LOG2E / TEACHER_TEMP)).astype(BF16)
            table[at_rows, at] = entry
            total = jnp.sum(entry.astype(F32).reshape(rows // 8, 8, tile), axis=0)
            acc8[:, at] = total if first else acc8[:, at] + total
            if last and (t + 1) % (TILES // PARTS) == 0:
                col_send_part(0, t // (TILES // PARTS))

    def student_block(xb):
        half_rows = sbuf[xb].astype(BF16)
        at_rows = pl.ds(pl.multiple_of(xb * rows, rows), rows)
        sht[:, at_rows] = jnp.transpose(sbuf[xb]).astype(BF16)
        wide = cols // 2
        total = None
        for t in range(2):
            at = pl.ds(t * wide, wide)
            dots = jnp.dot(half_rows, ph[:, at], preferred_element_type=F32)
            ex = jnp.exp2(dots * (LOG2E / STUDENT_TEMP))
            expo[at_rows, at] = ex
            for i in range(wide // LANES):
                piece = ex[:, i * LANES:(i + 1) * LANES]
                total = piece if total is None else total + piece
        sacc[at_rows, :] = total

    def half_arrived(buf, which, d):
        one = buf.at[0, pl.ds(0, half)]
        pltpu.make_async_copy(one, one, fw_recv.at[which, d - 1]).wait()

    teacher_block(x, first=True)
    student_block(x)
    for d in x_order:
        spread(tbuf, 0, d).wait_recv()
        forward(tbuf, 0, d).start()
    for d in x_order:
        spread(sbuf, 1, d).start()
    for d in x_order:
        half_arrived(tbuf, 0, d)
        teacher_block(xs[nx - d], last=d == x_order[-1])

    def student_forward():
        for d in x_order:
            spread(sbuf, 1, d).wait_recv()
            forward(sbuf, 1, d).start()

    def student_arrived(d):
        half_arrived(sbuf, 1, d)
        student_block(xs[nx - d])

    def pack(ref):
        parts = []
        for i in range(sz.packed):
            block = ref[i * LANES:(i + 1) * LANES, :]
            parts.append(jnp.sum(jnp.transpose(block), axis=0, keepdims=True))
        return jnp.concatenate(parts, axis=0)

    def unpack(value, ref):
        for i in range(sz.packed):
            block = jnp.broadcast_to(value[i:i + 1, :], (LANES, LANES))
            ref[i * LANES:(i + 1) * LANES, :] = jnp.transpose(block)

    def row_pass(q):
        @pl.loop(0, blocks)
        def _(b):
            at_rows = pl.ds(pl.multiple_of(b * BLOCK, BLOCK), BLOCK)
            acc = racc[at_rows, :] if q else None
            for j in range(part // LANES):
                at = pl.ds(q * part + j * LANES, LANES)
                term = table[at_rows, at].astype(F32) * colv[:, at]
                acc = term if acc is None else acc + term
            racc[at_rows, :] = acc

    def col_pass(q):
        acc8[:, pl.ds(q * part, part)] = jnp.zeros((8, part), F32)

        @pl.loop(0, blocks)
        def _(b):
            at_rows = pl.ds(pl.multiple_of(b * BLOCK, BLOCK), BLOCK)
            by_row = rscale[at_rows, :]
            for j in range(part // LANES):
                at = pl.ds(q * part + j * LANES, LANES)
                term = table[at_rows, at].astype(F32) * by_row
                acc8[:, at] += jnp.sum(term.reshape(BLOCK // 8, 8, LANES), axis=0)

    def row_exchange_start(sweep):
        for _, k, xx, yy, cc in group:
            pltpu.make_async_remote_copy(
                src_ref=rmsg[sweep],
                dst_ref=rbuf[sweep].at[k - 1],
                send_sem=row_send.at[sweep],
                recv_sem=row_recv.at[sweep],
                device_id=place(xx, z, yy, cc),
                device_id_type=MESH,
            ).start()

    def row_exchange_end(sweep):
        bulk_wait(rbuf[sweep], row_recv.at[sweep])
        return rmsg[sweep][...] + jnp.sum(rbuf[sweep][...], axis=0)

    for sweep in range(SWEEPS):
        if sweep > 0:
            for q in range(PARTS):
                col_pass(q)
                col_send_part(sweep, q)
        if sweep == 1:
            student_arrived(x_order[-1])
            rmsg[sweep][sz.packed:, :] = pack(sacc)
        for q in range(PARTS):
            col_recv_part(sweep, q)
            row_pass(q)
        rmsg[sweep][0:sz.packed, :] = pack(racc)
        row_exchange_start(sweep)
        if sweep == 0:
            student_forward()
            for d in x_order[:-1]:
                student_arrived(d)
        total = row_exchange_end(sweep)
        if sweep == 1:
            unpack((LOSS_SCALE / STUDENT_TEMP) / total[sz.packed:, :], sscale)
            total = total[0:sz.packed, :]
        if sweep == SWEEPS - 1:
            unpack((LOSS_SCALE / STUDENT_TEMP) / total, rscale)
        else:
            unpack(1.0 / total, rscale)

    def gradient_tile(t):
        at = pl.ds(t * tile, tile)

        @pl.loop(0, blocks)
        def _(b):
            at_rows = pl.ds(pl.multiple_of(b * BLOCK, BLOCK), BLOCK)
            by_row = sscale[at_rows, :]
            by_row_t = rscale[at_rows, :]
            for j in range(chunks):
                at_j = pl.ds(t * tile + j * LANES, LANES)
                target = (table[at_rows, at_j].astype(F32) * by_row_t) * colv[:, at_j]
                score = expo[at_rows, at_j] * by_row - target
                dbuf[at_rows, j * LANES:(j + 1) * LANES] = score.astype(BF16)

        pg = jnp.dot(sht[...], dbuf[...], preferred_element_type=F32)
        inv = winv[:, at]
        pu = wbuf[:, at].astype(F32) * inv
        dots = jnp.sum(pu * pg, axis=0, keepdims=True)
        out = (pg - pu * dots) * inv
        grad[:, :, :, at] = out.reshape(nx, nz, sz.bw, tile)

    def unit_tile(t):
        more = jnp.dot(dbuf[...], pht[pl.ds(t * tile, tile), :], preferred_element_type=F32)
        unit[...] = more if t == 0 else unit[...] + more

    def ring_block(stream, s):
        if stream % 2 == 0:
            return (z + 2 * nz - 1 - s) % nz
        return (z + 1 + s) % nz

    def ring_send_copy(stream, s, src):
        return pltpu.make_async_remote_copy(
            src_ref=src,
            dst_ref=ring.at[stream, s],
            send_sem=ring_send.at[stream, s],
            recv_sem=ring_recv.at[stream, s],
            device_id=place(x, zs[1 if stream % 2 == 0 else nz - 1], y, c),
            device_id_type=MESH,
        )

    def begin(stream):
        block = grad.at[:, ring_block(stream, 0), :, pl.ds(stream * tile, tile)]
        ring_send_copy(stream, 0, block).start()

    def serve(stream, s, last=False):
        slot = ring.at[stream, s]
        bulk_wait(slot, ring_recv.at[stream, s])
        at = pl.ds(stream * tile, tile)
        slot[...] = slot[...] + grad[:, ring_block(stream, s + 1), :, at]
        if not last:
            ring_send_copy(stream, s + 1, slot).start()

    def out_slice(stream):
        return gw_ref.at[:, pl.ds(pl.multiple_of(x * cols + stream * tile, tile), tile)]

    def own_copy(stream):
        return pltpu.make_async_copy(
            ring.at[stream, sz.steps - 1, x], out_slice(stream), own_sem.at[stream]
        )

    def deliver(stream):
        for d in range(1, nx):
            pltpu.make_async_remote_copy(
                src_ref=ring.at[stream, sz.steps - 1, xs[d]],
                dst_ref=out_slice(stream),
                send_sem=x_send.at[stream, d - 1],
                recv_sem=x_recv.at[stream, d - 1],
                device_id=place(xs[d], z, y, c),
                device_id_type=MESH,
            ).start()
        own_copy(stream).start()

    early = range(0, TILES // 2)
    late = range(TILES // 2, TILES)
    for t in range(TILES):
        gradient_tile(t)
        begin(t)
        unit_tile(t)
        if t >= TILES // 2 - 1 and t < TILES - 1:
            n = t - (TILES // 2 - 1)
            serve(n, 0, last=sz.steps == 1)

    for _, k, xx, yy, cc in group:
        first = xx * rows + (yy * nc + cc) * sz.share
        pltpu.make_async_remote_copy(
            src_ref=unit.at[pl.ds(pl.multiple_of(first, sz.share), sz.share)],
            dst_ref=ubuf.at[k - 1],
            send_sem=u_send,
            recv_sem=u_recv,
            device_id=place(xx, z, yy, cc),
            device_id_type=MESH,
        ).start()

    def ring_steps(first, last):
        @pl.loop(first, last)
        def _(s):
            for stream in early:
                serve(stream, s + 1)
            for stream in late:
                serve(stream, s)

    middle = max((sz.steps - 2) // 2, 0)
    ring_steps(0, middle)

    mine = pl.ds(pl.multiple_of((y * nc + c) * sz.share, sz.share), sz.share)
    bulk_wait(ubuf, u_recv)
    first = pl.multiple_of(x * rows + (y * nc + c) * sz.share, sz.share)
    total = unit[pl.ds(first, sz.share), :]
    for k in range(sz.group - 1):
        total = total + ubuf[k]
    unit_mine = sbuf[x, mine]
    along = jnp.sum(unit_mine * total, axis=1, keepdims=True)
    rowg[mine, :] = (total - unit_mine * along) / snorm[mine, 0:1]
    for k in range(1, ny * nc):
        pltpu.make_async_remote_copy(
            src_ref=rowg.at[mine],
            dst_ref=rowg.at[mine],
            send_sem=g_send,
            recv_sem=g_recv,
            device_id=place(x, z, ys[k // nc], cs[k % nc]),
            device_id_type=MESH,
        ).start()

    ring_steps(middle, sz.steps - 2)
    for stream in early:
        serve(stream, sz.steps - 1, last=True)
        deliver(stream)
    for stream in late:
        serve(stream, sz.steps - 2)
    for stream in late:
        serve(stream, sz.steps - 1, last=True)
        deliver(stream)

    others = pl.ds(0, rows - sz.share)
    bulk_wait(rowg.at[others], g_recv)
    bulk_wait(rowg.at[others], g_send)
    for which, buf in ((0, tbuf), (1, sbuf)):
        for d in range(1, nx):
            spread(buf, which, d).wait_send()
            forward(buf, which, d).wait_send()
    for sweep in range(SWEEPS):
        for q in range(PARTS):
            bulk_wait(colbuf.at[sweep, q], col_send.at[sweep, q])
        bulk_wait(rbuf[sweep], row_send.at[sweep])
    bulk_wait(ubuf, u_send)

    @pl.loop(0, sz.steps)
    def _(s):
        for stream in range(TILES):
            bulk_wait(ring.at[stream, s], ring_send.at[stream, s])

    for stream in range(TILES):
        own_copy(stream).wait()
        for d in range(1, nx):
            bulk_wait(ring.at[stream, 0, 0], x_send.at[stream, d - 1])
            bulk_wait(ring.at[stream, 0, 0], x_recv.at[stream, d - 1])


def finish(sz, mask_ref, rowg_ref, gw_in, gs_ref, gw_out):
    gw_out[...] = gw_in[...]
    at = lax.broadcasted_iota(jnp.int32, (sz.patches, sz.rows), 0)
    picks = jnp.where(at == mask_ref[...], 1.0, 0.0).astype(BF16)
    rest = rowg_ref[...]
    out = None
    for _ in range(3):
        piece = rest.astype(BF16)
        rest = rest - piece.astype(F32)
        term = jnp.dot(picks, piece, preferred_element_type=F32)
        out = term if out is None else out + term
    gs_ref[...] = out


def per_device(sz, student_patches, teacher_patches, weights_raw, masked_rows):
    vmem = pl.BlockSpec(memory_space=pltpu.VMEM)
    anywhere = pl.BlockSpec(memory_space=pl.ANY)
    dma = pltpu.SemaphoreType.DMA
    g = sz.group
    nx, nz = sz.nx, sz.nz
    p = sz.packed
    scratch = [
        pltpu.VMEM((sz.patches, sz.width), BF16),
        pltpu.VMEM((sz.patches, sz.width), BF16),
        pltpu.VMEM((sz.width, sz.cols), BF16),
        pltpu.VMEM((sz.width, sz.cols), BF16),
        pltpu.VMEM((sz.cols, sz.width), BF16),
        pltpu.VMEM((1, sz.cols), F32),
        pltpu.VMEM((nx, sz.rows, sz.width), F32),
        pltpu.VMEM((nx, sz.rows, sz.width), F32),
        pltpu.VMEM((sz.rows, LANES), F32),
        pltpu.VMEM((sz.width, sz.all_rows), BF16),
        pltpu.VMEM((sz.all_rows, sz.cols), BF16),
        pltpu.VMEM((sz.all_rows, sz.cols), F32),
        pltpu.VMEM((8, sz.cols), F32),
        pltpu.VMEM((1, sz.cols), F32),
        pltpu.VMEM((SWEEPS, PARTS, 1, sz.part), F32),
        pltpu.VMEM((SWEEPS, PARTS, nz - 1, 1, sz.part), F32),
        pltpu.VMEM((sz.all_rows, LANES), F32),
        pltpu.VMEM((sz.all_rows, LANES), F32),
        pltpu.VMEM((sz.all_rows, LANES), F32),
        pltpu.VMEM((sz.all_rows, LANES), F32),
        pltpu.VMEM((p, LANES), F32),
        pltpu.VMEM((2 * p, LANES), F32),
        pltpu.VMEM((p, LANES), F32),
        pltpu.VMEM((g - 1, p, LANES), F32),
        pltpu.VMEM((g - 1, 2 * p, LANES), F32),
        pltpu.VMEM((g - 1, p, LANES), F32),
        pltpu.VMEM((sz.all_rows, sz.tile), BF16),
        pltpu.VMEM((sz.all_rows, sz.width), F32),
        pltpu.VMEM((g - 1, sz.share, sz.width), F32),
        pltpu.VMEM((nx, nz, sz.bw, sz.cols), F32),
        pltpu.VMEM((TILES, sz.steps, nx, sz.bw, sz.tile), F32),
        dma((2,)),
        dma(()),
        dma((TILES,)),
        dma((2, nx - 1)),
        dma((2, nx - 1)),
        dma((2, nx - 1)),
        dma((2, nx - 1)),
        dma((SWEEPS, PARTS)),
        dma((SWEEPS, PARTS)),
        dma((SWEEPS,)),
        dma((SWEEPS,)),
        dma(()),
        dma(()),
        dma(()),
        dma(()),
        dma((TILES, sz.steps)),
        dma((TILES, sz.steps)),
        dma((TILES, nx - 1)),
        dma((TILES, nx - 1)),
    ]
    picked = masked_rows.reshape(1, sz.rows)
    row_grad, grad_weight = pl.pallas_call(
        functools.partial(kernel, sz),
        out_shape=(
            jax.ShapeDtypeStruct((sz.rows, sz.width), F32),
            jax.ShapeDtypeStruct((sz.bw, sz.cols_dp), F32),
        ),
        in_specs=[vmem, anywhere, anywhere, anywhere],
        out_specs=(vmem, anywhere),
        scratch_shapes=scratch,
        compiler_params=pltpu.CompilerParams(
            collective_id=0, has_side_effects=True, vmem_limit_bytes=56 * 1024 * 1024
        ),
        cost_estimate=pl.CostEstimate(
            flops=8 * sz.all_rows * sz.cols * sz.width,
            bytes_accessed=4 * sz.width * sz.cols,
            transcendentals=2 * sz.all_rows * sz.cols,
        ),
        name="sinkhorn_loss",
    )(picked, student_patches, teacher_patches, weights_raw)
    return pl.pallas_call(
        functools.partial(finish, sz),
        out_shape=(
            jax.ShapeDtypeStruct((sz.patches, sz.width), F32),
            jax.ShapeDtypeStruct((sz.bw, sz.cols_dp), F32),
        ),
        in_specs=[vmem, vmem, vmem],
        out_specs=(vmem, vmem),
        name="finish",
    )(picked, row_grad, grad_weight)


def solution(mesh):
    placed = (P("dp", None), P("dp", None), P(None, "proto"), P("dp"))
    mesh_shape = (mesh.shape["dp"], mesh.shape["proto"])

    def body(student_patches, teacher_patches, weights_raw, masked_rows):
        sz = Sizes(
            mesh_shape,
            weights_raw.shape[0],
            student_patches.shape[0],
            masked_rows.shape[0],
            weights_raw.shape[1],
        )
        return per_device(sz, student_patches, teacher_patches, weights_raw, masked_rows)

    return jax.shard_map(
        body,
        mesh=mesh,
        in_specs=placed,
        out_specs=(P("dp", None), P("dp", "proto")),
        check_vma=False,
    )
```

```python
import functools
import math

import jax
import jax.numpy as jnp
from jax import lax
from jax.experimental import pallas as pl
from jax.experimental.pallas import tpu as pltpu
from jax.sharding import PartitionSpec as P

MESH = pl.DeviceIdType.MESH
F32 = jnp.float32
BF16 = jnp.bfloat16
SWEEPS = 3
TEACHER_TEMP = 0.07
STUDENT_TEMP = 0.1
LOSS_SCALE = 2048.0
LOG2E = math.log2(math.e)
LANES = 128
TILES = 8
PARTS = 4
BLOCK = 128


class Sizes:
    def __init__(self, mesh_shape, width, patches, rows, protos):
        n_dp, n_proto = mesh_shape
        self.nc = 2
        self.ny = n_proto // 2
        self.nx = 4 if n_dp >= 16 else 2
        self.nz = n_dp // self.nx
        self.width = width
        self.patches = patches
        self.rows = rows
        self.all_rows = rows * self.nx
        self.cols_dp = protos
        self.cols = protos // self.nx
        self.tile = self.cols // TILES
        self.part = self.cols // PARTS
        self.bw = width // n_dp
        self.group = self.nx * self.ny * self.nc
        self.packed = self.all_rows // LANES
        self.share = rows // (self.ny * self.nc)
        self.steps = self.nz - 1


def bulk_wait(ref, sem):
    pltpu.make_async_copy(ref, ref, sem).wait()


def ring_distance(step, size):
    return min(step, size - step)


def kernel(
    sz, mask_ref, stu_hbm, tea_hbm, w_hbm, rowg, gw_ref,
    stu_ref, tea_ref, wbuf, ph, pht, winv, tbuf, sbuf, snorm, sht, table, expo,
    acc8, colv, colmsg, colbuf, racc, sacc, rscale, sscale,
    rmsg0, rmsg1, rmsg2, rbuf0, rbuf1, rbuf2,
    unit, ubuf, grad, ring,
    in_sem, w_sem, own_sem, ts_send, ts_recv, fw_send, fw_recv, col_send, col_recv,
    row_send, row_recv, u_send, u_recv, g_send, g_recv, ring_send, ring_recv, x_send, x_recv,
):
    nx, ny, nc, nz = sz.nx, sz.ny, sz.nc, sz.nz
    rows, cols, tile, part = sz.rows, sz.cols, sz.tile, sz.part
    chunks = tile // LANES
    blocks = sz.all_rows // BLOCK
    rmsg = (rmsg0, rmsg1, rmsg2)
    rbuf = (rbuf0, rbuf1, rbuf2)
    dp = lax.axis_index("dp")
    pr = lax.axis_index("proto")
    x, z = dp // nz, dp % nz
    y, c = pr // nc, pr % nc
    half = rows // nc

    xs = [x] + [(x + d) % nx for d in range(1, nx)]
    ys = [y] + [(y + d) % ny for d in range(1, ny)]
    cs = [c] + [(c + d) % nc for d in range(1, nc)]
    zs = [z] + [(z + d) % nz for d in range(1, nz)]

    def place(xx, zz, yy, cc):
        return (xx * nz + zz, yy * nc + cc)

    group = []
    for k in range(1, sz.group):
        dx, dy, dc = k // (ny * nc), (k // nc) % ny, k % nc
        far = ring_distance(dx, nx) + ring_distance(dy, ny)
        group.append((-far, k, xs[dx], ys[dy], cs[dc]))
    group.sort(key=lambda entry: entry[:2])
    z_order = sorted(range(1, nz), key=lambda d: -ring_distance(d, nz))

    barrier = pltpu.get_barrier_semaphore()
    for _, _, xx, yy, cc in group:
        pl.semaphore_signal(barrier, inc=1, device_id=place(xx, z, yy, cc), device_id_type=MESH)
    for d in z_order:
        pl.semaphore_signal(barrier, inc=1, device_id=place(x, zs[d], y, c), device_id_type=MESH)

    tea_copy = pltpu.make_async_copy(tea_hbm, tea_ref, in_sem.at[0])
    stu_copy = pltpu.make_async_copy(stu_hbm, stu_ref, in_sem.at[1])
    w_copy = pltpu.make_async_copy(
        w_hbm.at[:, pl.ds(pl.multiple_of(x * cols, cols), cols)], wbuf, w_sem
    )
    tea_copy.start()
    stu_copy.start()
    w_copy.start()

    at = lax.broadcasted_iota(jnp.int32, (sz.patches, rows), 0)
    one_hot_t = jnp.where(at == mask_ref[...], 1.0, 0.0).astype(BF16)

    def unit_rows(ref):
        picked = lax.dot_general(
            one_hot_t, ref[...], (((0,), (0,)), ((), ())), preferred_element_type=F32
        )
        norm = jnp.sqrt(jnp.sum(picked * picked, axis=1, keepdims=True) + 1e-06)
        return picked / norm, norm

    tea_copy.wait()
    tbuf[x] = unit_rows(tea_ref)[0]
    stu_copy.wait()
    stu_unit, stu_norm = unit_rows(stu_ref)
    sbuf[x] = stu_unit
    snorm[...] = jnp.broadcast_to(stu_norm, (rows, LANES))

    pl.semaphore_wait(barrier, sz.group - 1 + nz - 1)

    my_half = pl.ds(pl.multiple_of(c * half, half), half)

    def spread(buf, which, d):
        return pltpu.make_async_remote_copy(
            src_ref=buf.at[x, my_half],
            dst_ref=buf.at[x, my_half],
            send_sem=ts_send.at[which, d - 1],
            recv_sem=ts_recv.at[which, d - 1],
            device_id=place(xs[d], z, y, c),
            device_id_type=MESH,
        )

    def forward(buf, which, d):
        return pltpu.make_async_remote_copy(
            src_ref=buf.at[xs[nx - d], my_half],
            dst_ref=buf.at[xs[nx - d], my_half],
            send_sem=fw_send.at[which, d - 1],
            recv_sem=fw_recv.at[which, d - 1],
            device_id=place(x, z, y, cs[1]),
            device_id_type=MESH,
        )

    x_order = sorted(range(1, nx), key=lambda d: ring_distance(d, nx))
    for d in x_order:
        spread(tbuf, 0, d).start()

    w_copy.wait()
    for t in range(TILES):
        at = pl.ds(t * tile, tile)
        w = wbuf[:, at].astype(F32)
        inv = 1.0 / jnp.sqrt(jnp.sum(w * w, axis=0, keepdims=True) + 1e-06)
        winv[:, at] = inv
        proto = (w * inv).astype(BF16)
        ph[:, at] = proto
        pht[at, :] = jnp.transpose(proto)

    def col_send_part(sweep, q):
        at = pl.ds(q * part, part)
        colmsg[sweep, q] = jnp.sum(acc8[:, at], axis=0, keepdims=True)
        for d in z_order:
            pltpu.make_async_remote_copy(
                src_ref=colmsg.at[sweep, q],
                dst_ref=colbuf.at[sweep, q, d - 1],
                send_sem=col_send.at[sweep, q],
                recv_sem=col_recv.at[sweep, q],
                device_id=place(x, zs[d], y, c),
                device_id_type=MESH,
            ).start()

    def col_recv_part(sweep, q):
        bulk_wait(colbuf.at[sweep, q], col_recv.at[sweep, q])
        total = colmsg[sweep, q]
        for k in range(nz - 1):
            total = total + colbuf[sweep, q, k]
        colv[:, pl.ds(q * part, part)] = 1.0 / total

    def teacher_block(xb, first=False, last=False):
        half_rows = tbuf[xb].astype(BF16)
        at_rows = pl.ds(pl.multiple_of(xb * rows, rows), rows)
        for t in range(TILES):
            at = pl.ds(t * tile, tile)
            dots = jnp.dot(half_rows, ph[:, at], preferred_element_type=F32)
            entry = jnp.exp2(dots * (LOG2E / TEACHER_TEMP)).astype(BF16)
            table[at_rows, at] = entry
            total = jnp.sum(entry.astype(F32).reshape(rows // 8, 8, tile), axis=0)
            acc8[:, at] = total if first else acc8[:, at] + total
            if last and (t + 1) % (TILES // PARTS) == 0:
                col_send_part(0, t // (TILES // PARTS))

    def student_block(xb):
        half_rows = sbuf[xb].astype(BF16)
        at_rows = pl.ds(pl.multiple_of(xb * rows, rows), rows)
        sht[:, at_rows] = jnp.transpose(sbuf[xb]).astype(BF16)
        wide = cols // 2
        total = None
        for t in range(2):
            at = pl.ds(t * wide, wide)
            dots = jnp.dot(half_rows, ph[:, at], preferred_element_type=F32)
            ex = jnp.exp2(dots * (LOG2E / STUDENT_TEMP))
            expo[at_rows, at] = ex
            for i in range(wide // LANES):
                piece = ex[:, i * LANES:(i + 1) * LANES]
                total = piece if total is None else total + piece
        sacc[at_rows, :] = total

    def half_arrived(buf, which, d):
        one = buf.at[0, pl.ds(0, half)]
        pltpu.make_async_copy(one, one, fw_recv.at[which, d - 1]).wait()

    teacher_block(x, first=True)
    student_block(x)
    for d in x_order[:2]:
        spread(tbuf, 0, d).wait_recv()
        forward(tbuf, 0, d).start()
    for n, d in enumerate(x_order):
        half_arrived(tbuf, 0, d)
        if n + 2 < nx - 1:
            teacher_block(xs[nx - d])
            spread(tbuf, 0, x_order[n + 2]).wait_recv()
            forward(tbuf, 0, x_order[n + 2]).start()
        if n == max(nx - 4, 0):
            for e in x_order:
                spread(sbuf, 1, e).start()
        if n + 2 >= nx - 1:
            teacher_block(xs[nx - d], last=d == x_order[-1])

    def student_forward():
        for d in x_order:
            spread(sbuf, 1, d).wait_recv()
            forward(sbuf, 1, d).start()

    def student_arrived(d):
        half_arrived(sbuf, 1, d)
        student_block(xs[nx - d])

    def pack(ref):
        parts = []
        for i in range(sz.packed):
            block = ref[i * LANES:(i + 1) * LANES, :]
            parts.append(jnp.sum(jnp.transpose(block), axis=0, keepdims=True))
        return jnp.concatenate(parts, axis=0)

    def unpack(value, ref):
        for i in range(sz.packed):
            block = jnp.broadcast_to(value[i:i + 1, :], (LANES, LANES))
            ref[i * LANES:(i + 1) * LANES, :] = jnp.transpose(block)

    def row_pass(q):
        @pl.loop(0, blocks)
        def _(b):
            at_rows = pl.ds(pl.multiple_of(b * BLOCK, BLOCK), BLOCK)
            acc = racc[at_rows, :] if q else None
            for j in range(part // LANES):
                at = pl.ds(q * part + j * LANES, LANES)
                term = table[at_rows, at].astype(F32) * colv[:, at]
                acc = term if acc is None else acc + term
            racc[at_rows, :] = acc

    def col_pass(q):
        acc8[:, pl.ds(q * part, part)] = jnp.zeros((8, part), F32)

        @pl.loop(0, blocks)
        def _(b):
            at_rows = pl.ds(pl.multiple_of(b * BLOCK, BLOCK), BLOCK)
            by_row = rscale[at_rows, :]
            for j in range(part // LANES):
                at = pl.ds(q * part + j * LANES, LANES)
                term = table[at_rows, at].astype(F32) * by_row
                acc8[:, at] += jnp.sum(term.reshape(BLOCK // 8, 8, LANES), axis=0)

    def row_exchange_start(sweep):
        for _, k, xx, yy, cc in group:
            pltpu.make_async_remote_copy(
                src_ref=rmsg[sweep],
                dst_ref=rbuf[sweep].at[k - 1],
                send_sem=row_send.at[sweep],
                recv_sem=row_recv.at[sweep],
                device_id=place(xx, z, yy, cc),
                device_id_type=MESH,
            ).start()

    def row_exchange_end(sweep):
        bulk_wait(rbuf[sweep], row_recv.at[sweep])
        return rmsg[sweep][...] + jnp.sum(rbuf[sweep][...], axis=0)

    def scale_probs():
        @pl.loop(0, blocks)
        def _(b):
            at_rows = pl.ds(pl.multiple_of(b * BLOCK, BLOCK), BLOCK)
            by_row = sscale[at_rows, :]
            for j in range(cols // LANES):
                at = pl.ds(j * LANES, LANES)
                expo[at_rows, at] = expo[at_rows, at] * by_row

    for sweep in range(SWEEPS):
        if sweep > 0:
            for q in range(PARTS):
                col_pass(q)
                col_send_part(sweep, q)
        if sweep == 1:
            student_arrived(x_order[-1])
            rmsg[sweep][sz.packed:, :] = pack(sacc)
        for q in range(PARTS):
            col_recv_part(sweep, q)
            row_pass(q)
        rmsg[sweep][0:sz.packed, :] = pack(racc)
        row_exchange_start(sweep)
        if sweep == 0:
            student_forward()
            for d in x_order[:-1]:
                student_arrived(d)
        if sweep == SWEEPS - 1:
            scale_probs()
        total = row_exchange_end(sweep)
        if sweep == 1:
            unpack((LOSS_SCALE / STUDENT_TEMP) / total[sz.packed:, :], sscale)
            total = total[0:sz.packed, :]
        if sweep == SWEEPS - 1:
            unpack((LOSS_SCALE / STUDENT_TEMP) / total, rscale)
        else:
            unpack(1.0 / total, rscale)

    def gradient_tile(t):
        at = pl.ds(t * tile, tile)

        @pl.loop(0, blocks)
        def _(b):
            at_rows = pl.ds(pl.multiple_of(b * BLOCK, BLOCK), BLOCK)
            by_row = rscale[at_rows, :]
            for j in range(chunks):
                at_j = pl.ds(t * tile + j * LANES, LANES)
                target = (table[at_rows, at_j].astype(F32) * by_row) * colv[:, at_j]
                table[at_rows, at_j] = (expo[at_rows, at_j] - target).astype(BF16)

        pg = jnp.dot(sht[...], table[:, at], preferred_element_type=F32)
        inv = winv[:, at]
        pu = wbuf[:, at].astype(F32) * inv
        dots = jnp.sum(pu * pg, axis=0, keepdims=True)
        out = (pg - pu * dots) * inv
        grad[:, :, :, at] = out.reshape(nx, nz, sz.bw, tile)

    def unit_tile(t):
        at = pl.ds(t * tile, tile)
        more = jnp.dot(table[:, at], pht[at, :], preferred_element_type=F32)
        unit[...] = more if t == 0 else unit[...] + more

    def ring_block(stream, s):
        if stream % 2 == 0:
            return (z + 2 * nz - 1 - s) % nz
        return (z + 1 + s) % nz

    def ring_send_copy(stream, s, src):
        return pltpu.make_async_remote_copy(
            src_ref=src,
            dst_ref=ring.at[stream, s],
            send_sem=ring_send.at[stream, s],
            recv_sem=ring_recv.at[stream, s],
            device_id=place(x, zs[1 if stream % 2 == 0 else nz - 1], y, c),
            device_id_type=MESH,
        )

    def begin(stream):
        block = grad.at[:, ring_block(stream, 0), :, pl.ds(stream * tile, tile)]
        ring_send_copy(stream, 0, block).start()

    def serve(stream, s, last=False):
        slot = ring.at[stream, s]
        bulk_wait(slot, ring_recv.at[stream, s])
        at = pl.ds(stream * tile, tile)
        slot[...] = slot[...] + grad[:, ring_block(stream, s + 1), :, at]
        if not last:
            ring_send_copy(stream, s + 1, slot).start()

    def out_slice(stream):
        return gw_ref.at[:, pl.ds(pl.multiple_of(x * cols + stream * tile, tile), tile)]

    def own_copy(stream):
        return pltpu.make_async_copy(
            ring.at[stream, sz.steps - 1, x], out_slice(stream), own_sem.at[stream]
        )

    def deliver(stream):
        for d in range(1, nx):
            pltpu.make_async_remote_copy(
                src_ref=ring.at[stream, sz.steps - 1, xs[d]],
                dst_ref=out_slice(stream),
                send_sem=x_send.at[stream, d - 1],
                recv_sem=x_recv.at[stream, d - 1],
                device_id=place(xs[d], z, y, c),
                device_id_type=MESH,
            ).start()
        own_copy(stream).start()

    early = range(0, TILES // 2)
    late = range(TILES // 2, TILES)
    for t in range(TILES):
        gradient_tile(t)
        begin(t)
        if t in late:
            serve(t - len(early), 0)
    for t in range(TILES):
        unit_tile(t)
        if t in early:
            serve(t + len(early), 0)
        else:
            serve(t - len(early), 1)

    for _, k, xx, yy, cc in group:
        first = xx * rows + (yy * nc + cc) * sz.share
        pltpu.make_async_remote_copy(
            src_ref=unit.at[pl.ds(pl.multiple_of(first, sz.share), sz.share)],
            dst_ref=ubuf.at[k - 1],
            send_sem=u_send,
            recv_sem=u_recv,
            device_id=place(xx, z, yy, cc),
            device_id_type=MESH,
        ).start()

    def ring_steps(first, last):
        @pl.loop(first, last)
        def _(s):
            for stream in late:
                serve(stream, s)
            for stream in early:
                serve(stream, s + 1)

    middle = max(sz.steps - 3, 1)
    ring_steps(1, middle)

    mine = pl.ds(pl.multiple_of((y * nc + c) * sz.share, sz.share), sz.share)
    bulk_wait(ubuf, u_recv)
    first = pl.multiple_of(x * rows + (y * nc + c) * sz.share, sz.share)
    total = unit[pl.ds(first, sz.share), :]
    for k in range(sz.group - 1):
        total = total + ubuf[k]
    unit_mine = sbuf[x, mine]
    along = jnp.sum(unit_mine * total, axis=1, keepdims=True)
    rowg[mine, :] = (total - unit_mine * along) / snorm[mine, 0:1]
    for k in range(1, ny * nc):
        pltpu.make_async_remote_copy(
            src_ref=rowg.at[mine],
            dst_ref=rowg.at[mine],
            send_sem=g_send,
            recv_sem=g_recv,
            device_id=place(x, z, ys[k // nc], cs[k % nc]),
            device_id_type=MESH,
        ).start()

    ring_steps(middle, sz.steps - 2)
    for stream in late:
        serve(stream, sz.steps - 2)
    for stream in early:
        serve(stream, sz.steps - 1, last=True)
        deliver(stream)
    for stream in late:
        serve(stream, sz.steps - 1, last=True)
        deliver(stream)

    others = pl.ds(0, rows - sz.share)
    bulk_wait(rowg.at[others], g_recv)
    bulk_wait(rowg.at[others], g_send)
    for which, buf in ((0, tbuf), (1, sbuf)):
        for d in range(1, nx):
            spread(buf, which, d).wait_send()
            forward(buf, which, d).wait_send()
    for sweep in range(SWEEPS):
        for q in range(PARTS):
            bulk_wait(colbuf.at[sweep, q], col_send.at[sweep, q])
        bulk_wait(rbuf[sweep], row_send.at[sweep])
    bulk_wait(ubuf, u_send)

    @pl.loop(0, sz.steps)
    def _(s):
        for stream in range(TILES):
            bulk_wait(ring.at[stream, s], ring_send.at[stream, s])

    for stream in range(TILES):
        own_copy(stream).wait()
        for d in range(1, nx):
            bulk_wait(ring.at[stream, 0, 0], x_send.at[stream, d - 1])
            bulk_wait(ring.at[stream, 0, 0], x_recv.at[stream, d - 1])


def finish(sz, mask_ref, rowg_ref, gw_in, gs_ref, gw_out):
    gw_out[...] = gw_in[...]
    at = lax.broadcasted_iota(jnp.int32, (sz.patches, sz.rows), 0)
    picks = jnp.where(at == mask_ref[...], 1.0, 0.0).astype(BF16)
    rest = rowg_ref[...]
    out = None
    for _ in range(3):
        piece = rest.astype(BF16)
        rest = rest - piece.astype(F32)
        term = jnp.dot(picks, piece, preferred_element_type=F32)
        out = term if out is None else out + term
    gs_ref[...] = out


def per_device(sz, student_patches, teacher_patches, weights_raw, masked_rows):
    vmem = pl.BlockSpec(memory_space=pltpu.VMEM)
    anywhere = pl.BlockSpec(memory_space=pl.ANY)
    dma = pltpu.SemaphoreType.DMA
    g = sz.group
    nx, nz = sz.nx, sz.nz
    p = sz.packed
    scratch = [
        pltpu.VMEM((sz.patches, sz.width), BF16),
        pltpu.VMEM((sz.patches, sz.width), BF16),
        pltpu.VMEM((sz.width, sz.cols), BF16),
        pltpu.VMEM((sz.width, sz.cols), BF16),
        pltpu.VMEM((sz.cols, sz.width), BF16),
        pltpu.VMEM((1, sz.cols), F32),
        pltpu.VMEM((nx, sz.rows, sz.width), F32),
        pltpu.VMEM((nx, sz.rows, sz.width), F32),
        pltpu.VMEM((sz.rows, LANES), F32),
        pltpu.VMEM((sz.width, sz.all_rows), BF16),
        pltpu.VMEM((sz.all_rows, sz.cols), BF16),
        pltpu.VMEM((sz.all_rows, sz.cols), F32),
        pltpu.VMEM((8, sz.cols), F32),
        pltpu.VMEM((1, sz.cols), F32),
        pltpu.VMEM((SWEEPS, PARTS, 1, sz.part), F32),
        pltpu.VMEM((SWEEPS, PARTS, nz - 1, 1, sz.part), F32),
        pltpu.VMEM((sz.all_rows, LANES), F32),
        pltpu.VMEM((sz.all_rows, LANES), F32),
        pltpu.VMEM((sz.all_rows, LANES), F32),
        pltpu.VMEM((sz.all_rows, LANES), F32),
        pltpu.VMEM((p, LANES), F32),
        pltpu.VMEM((2 * p, LANES), F32),
        pltpu.VMEM((p, LANES), F32),
        pltpu.VMEM((g - 1, p, LANES), F32),
        pltpu.VMEM((g - 1, 2 * p, LANES), F32),
        pltpu.VMEM((g - 1, p, LANES), F32),
        pltpu.VMEM((sz.all_rows, sz.width), F32),
        pltpu.VMEM((g - 1, sz.share, sz.width), F32),
        pltpu.VMEM((nx, nz, sz.bw, sz.cols), F32),
        pltpu.VMEM((TILES, sz.steps, nx, sz.bw, sz.tile), F32),
        dma((2,)),
        dma(()),
        dma((TILES,)),
        dma((2, nx - 1)),
        dma((2, nx - 1)),
        dma((2, nx - 1)),
        dma((2, nx - 1)),
        dma((SWEEPS, PARTS)),
        dma((SWEEPS, PARTS)),
        dma((SWEEPS,)),
        dma((SWEEPS,)),
        dma(()),
        dma(()),
        dma(()),
        dma(()),
        dma((TILES, sz.steps)),
        dma((TILES, sz.steps)),
        dma((TILES, nx - 1)),
        dma((TILES, nx - 1)),
    ]
    picked = masked_rows.reshape(1, sz.rows)
    row_grad, grad_weight = pl.pallas_call(
        functools.partial(kernel, sz),
        out_shape=(
            jax.ShapeDtypeStruct((sz.rows, sz.width), F32),
            jax.ShapeDtypeStruct((sz.bw, sz.cols_dp), F32),
        ),
        in_specs=[vmem, anywhere, anywhere, anywhere],
        out_specs=(vmem, anywhere),
        scratch_shapes=scratch,
        compiler_params=pltpu.CompilerParams(
            collective_id=0, has_side_effects=True, vmem_limit_bytes=56 * 1024 * 1024
        ),
        cost_estimate=pl.CostEstimate(
            flops=8 * sz.all_rows * sz.cols * sz.width,
            bytes_accessed=4 * sz.width * sz.cols,
            transcendentals=2 * sz.all_rows * sz.cols,
        ),
        name="sinkhorn_loss",
    )(picked, student_patches, teacher_patches, weights_raw)
    return pl.pallas_call(
        functools.partial(finish, sz),
        out_shape=(
            jax.ShapeDtypeStruct((sz.patches, sz.width), F32),
            jax.ShapeDtypeStruct((sz.bw, sz.cols_dp), F32),
        ),
        in_specs=[vmem, vmem, vmem],
        out_specs=(vmem, vmem),
        name="finish",
    )(picked, row_grad, grad_weight)


def solution(mesh):
    placed = (P("dp", None), P("dp", None), P(None, "proto"), P("dp"))
    mesh_shape = (mesh.shape["dp"], mesh.shape["proto"])

    def body(student_patches, teacher_patches, weights_raw, masked_rows):
        sz = Sizes(
            mesh_shape,
            weights_raw.shape[0],
            student_patches.shape[0],
            masked_rows.shape[0],
            weights_raw.shape[1],
        )
        return per_device(sz, student_patches, teacher_patches, weights_raw, masked_rows)

    return jax.shard_map(
        body,
        mesh=mesh,
        in_specs=placed,
        out_specs=(P("dp", None), P("dp", "proto")),
        check_vma=False,
    )
```

```python
import functools
import math

import jax
import jax.numpy as jnp
from jax import lax
from jax.experimental import pallas as pl
from jax.experimental.pallas import tpu as pltpu
from jax.sharding import PartitionSpec as P

MESH = pl.DeviceIdType.MESH
F32 = jnp.float32
BF16 = jnp.bfloat16
SWEEPS = 3
TEACHER_TEMP = 0.07
STUDENT_TEMP = 0.1
LOSS_SCALE = 2048.0
LOG2E = math.log2(math.e)
LANES = 128
TILES = 8
PARTS = 4
BLOCK = 128


class Sizes:
    def __init__(self, mesh_shape, width, patches, rows, protos):
        n_dp, n_proto = mesh_shape
        self.nc = 2
        self.ny = n_proto // 2
        self.nx = 4 if n_dp >= 16 else 2
        self.nz = n_dp // self.nx
        self.width = width
        self.patches = patches
        self.rows = rows
        self.all_rows = rows * self.nx
        self.cols_dp = protos
        self.cols = protos // self.nx
        self.tile = self.cols // TILES
        self.part = self.cols // PARTS
        self.bw = width // n_dp
        self.group = self.nx * self.ny * self.nc
        self.packed = self.all_rows // LANES
        self.share = rows // (self.ny * self.nc)
        self.steps = self.nz - 1


def bulk_wait(ref, sem):
    pltpu.make_async_copy(ref, ref, sem).wait()


def ring_distance(step, size):
    return min(step, size - step)


def kernel(
    sz, mask_ref, stu_hbm, tea_hbm, w_hbm, rowg, gw_ref,
    stu_ref, tea_ref, wbuf, ph, pht, winv, tbuf, sbuf, snorm, sht, table, expo,
    acc8, colv, colmsg, colbuf, racc, sacc, rscale, sscale,
    rmsg0, rmsg1, rmsg2, rbuf0, rbuf1, rbuf2,
    unit, ubuf, grad, ring,
    in_sem, w_sem, own_sem, ts_send, ts_recv, rl_send, rl_recv, fw_send, fw_recv,
    col_send, col_recv,
    row_send, row_recv, u_send, u_recv, g_send, g_recv, ring_send, ring_recv, x_send, x_recv,
):
    nx, ny, nc, nz = sz.nx, sz.ny, sz.nc, sz.nz
    rows, cols, tile, part = sz.rows, sz.cols, sz.tile, sz.part
    chunks = tile // LANES
    blocks = sz.all_rows // BLOCK
    rmsg = (rmsg0, rmsg1, rmsg2)
    rbuf = (rbuf0, rbuf1, rbuf2)
    dp = lax.axis_index("dp")
    pr = lax.axis_index("proto")
    x, z = dp // nz, dp % nz
    y, c = pr // nc, pr % nc
    half = rows // nc

    xs = [x] + [(x + d) % nx for d in range(1, nx)]
    ys = [y] + [(y + d) % ny for d in range(1, ny)]
    cs = [c] + [(c + d) % nc for d in range(1, nc)]
    zs = [z] + [(z + d) % nz for d in range(1, nz)]

    def place(xx, zz, yy, cc):
        return (xx * nz + zz, yy * nc + cc)

    group = []
    for k in range(1, sz.group):
        dx, dy, dc = k // (ny * nc), (k // nc) % ny, k % nc
        far = ring_distance(dx, nx) + ring_distance(dy, ny)
        group.append((-far, k, xs[dx], ys[dy], cs[dc]))
    group.sort(key=lambda entry: entry[:2])
    z_order = sorted(range(1, nz), key=lambda d: -ring_distance(d, nz))

    barrier = pltpu.get_barrier_semaphore()
    for _, _, xx, yy, cc in group:
        pl.semaphore_signal(barrier, inc=1, device_id=place(xx, z, yy, cc), device_id_type=MESH)
    for d in z_order:
        pl.semaphore_signal(barrier, inc=1, device_id=place(x, zs[d], y, c), device_id_type=MESH)

    tea_copy = pltpu.make_async_copy(tea_hbm, tea_ref, in_sem.at[0])
    stu_copy = pltpu.make_async_copy(stu_hbm, stu_ref, in_sem.at[1])
    w_copy = pltpu.make_async_copy(
        w_hbm.at[:, pl.ds(pl.multiple_of(x * cols, cols), cols)], wbuf, w_sem
    )
    tea_copy.start()
    stu_copy.start()
    w_copy.start()

    at = lax.broadcasted_iota(jnp.int32, (sz.patches, rows), 0)
    one_hot_t = jnp.where(at == mask_ref[...], 1.0, 0.0).astype(BF16)

    def unit_rows(ref):
        picked = lax.dot_general(
            one_hot_t, ref[...], (((0,), (0,)), ((), ())), preferred_element_type=F32
        )
        norm = jnp.sqrt(jnp.sum(picked * picked, axis=1, keepdims=True) + 1e-06)
        return picked / norm, norm

    tea_copy.wait()
    tbuf[x] = unit_rows(tea_ref)[0]
    stu_copy.wait()
    stu_unit, stu_norm = unit_rows(stu_ref)
    sbuf[x] = stu_unit
    snorm[...] = jnp.broadcast_to(stu_norm, (rows, LANES))

    pl.semaphore_wait(barrier, sz.group - 1 + nz - 1)

    my_half = pl.ds(pl.multiple_of(c * half, half), half)

    def spread(buf, which, d):
        return pltpu.make_async_remote_copy(
            src_ref=buf.at[x, my_half],
            dst_ref=buf.at[x, my_half],
            send_sem=ts_send.at[which, d - 1],
            recv_sem=ts_recv.at[which, d - 1],
            device_id=place(xs[d], z, y, c),
            device_id_type=MESH,
        )

    def forward(buf, which, d):
        return pltpu.make_async_remote_copy(
            src_ref=buf.at[xs[nx - d], my_half],
            dst_ref=buf.at[xs[nx - d], my_half],
            send_sem=fw_send.at[which, d - 1],
            recv_sem=fw_recv.at[which, d - 1],
            device_id=place(x, z, y, cs[1]),
            device_id_type=MESH,
        )

    x_order = sorted(range(1, nx), key=lambda d: ring_distance(d, nx))
    for d in x_order[:2]:
        spread(tbuf, 0, d).start()

    w_copy.wait()
    for t in range(TILES):
        at = pl.ds(t * tile, tile)
        w = wbuf[:, at].astype(F32)
        inv = 1.0 / jnp.sqrt(jnp.sum(w * w, axis=0, keepdims=True) + 1e-06)
        winv[:, at] = inv
        proto = (w * inv).astype(BF16)
        ph[:, at] = proto
        pht[at, :] = jnp.transpose(proto)

    def col_send_part(sweep, q):
        at = pl.ds(q * part, part)
        colmsg[sweep, q] = jnp.sum(acc8[:, at], axis=0, keepdims=True)
        for d in z_order:
            pltpu.make_async_remote_copy(
                src_ref=colmsg.at[sweep, q],
                dst_ref=colbuf.at[sweep, q, d - 1],
                send_sem=col_send.at[sweep, q],
                recv_sem=col_recv.at[sweep, q],
                device_id=place(x, zs[d], y, c),
                device_id_type=MESH,
            ).start()

    def col_recv_part(sweep, q):
        bulk_wait(colbuf.at[sweep, q], col_recv.at[sweep, q])
        total = colmsg[sweep, q]
        for k in range(nz - 1):
            total = total + colbuf[sweep, q, k]
        colv[:, pl.ds(q * part, part)] = 1.0 / total

    def teacher_block(xb, first=False, last=False):
        half_rows = tbuf[xb].astype(BF16)
        at_rows = pl.ds(pl.multiple_of(xb * rows, rows), rows)
        for t in range(TILES):
            at = pl.ds(t * tile, tile)
            dots = jnp.dot(half_rows, ph[:, at], preferred_element_type=F32)
            entry = jnp.exp2(dots * (LOG2E / TEACHER_TEMP)).astype(BF16)
            table[at_rows, at] = entry
            total = jnp.sum(entry.astype(F32).reshape(rows // 8, 8, tile), axis=0)
            acc8[:, at] = total if first else acc8[:, at] + total
            if last and (t + 1) % (TILES // PARTS) == 0:
                col_send_part(0, t // (TILES // PARTS))

    def student_block(xb):
        half_rows = sbuf[xb].astype(BF16)
        at_rows = pl.ds(pl.multiple_of(xb * rows, rows), rows)
        sht[:, at_rows] = jnp.transpose(sbuf[xb]).astype(BF16)
        wide = cols // 2
        total = None
        for t in range(2):
            at = pl.ds(t * wide, wide)
            dots = jnp.dot(half_rows, ph[:, at], preferred_element_type=F32)
            ex = jnp.exp2(dots * (LOG2E / STUDENT_TEMP))
            expo[at_rows, at] = ex
            for i in range(wide // LANES):
                piece = ex[:, i * LANES:(i + 1) * LANES]
                total = piece if total is None else total + piece
        sacc[at_rows, :] = total

    def half_arrived(buf, which, d):
        one = buf.at[0, pl.ds(0, half)]
        pltpu.make_async_copy(one, one, fw_recv.at[which, d - 1]).wait()

    quarter = half // 2

    def relay(n):
        block = xs[nx - 1] if n == 0 else xs[1]
        piece = tbuf.at[block, pl.ds(pl.multiple_of(c * half + n * quarter, quarter), quarter)]
        return pltpu.make_async_remote_copy(
            src_ref=piece,
            dst_ref=piece,
            send_sem=rl_send.at[n],
            recv_sem=rl_recv.at[n],
            device_id=place(xs[1] if n == 0 else xs[nx - 1], z, y, c),
            device_id_type=MESH,
        )

    near = x_order[:2]
    far = x_order[2:]
    teacher_block(x, first=True)
    for n, d in enumerate(near):
        spread(tbuf, 0, d).wait_recv()
        if far:
            relay(n).start()
        forward(tbuf, 0, d).start()
    student_block(x)
    for d in near:
        half_arrived(tbuf, 0, d)
        teacher_block(xs[nx - d], last=d == x_order[-1])
    if far:
        relay(0).wait_recv()
        relay(1).wait_recv()
        forward(tbuf, 0, far[0]).start()
    for d in x_order:
        spread(sbuf, 1, d).start()
    for d in far:
        half_arrived(tbuf, 0, d)
        teacher_block(xs[nx - d], last=True)

    def student_forward():
        for d in x_order:
            spread(sbuf, 1, d).wait_recv()
            forward(sbuf, 1, d).start()

    def student_arrived(d):
        half_arrived(sbuf, 1, d)
        student_block(xs[nx - d])

    def pack(ref):
        parts = []
        for i in range(sz.packed):
            block = ref[i * LANES:(i + 1) * LANES, :]
            parts.append(jnp.sum(jnp.transpose(block), axis=0, keepdims=True))
        return jnp.concatenate(parts, axis=0)

    def unpack(value, ref):
        for i in range(sz.packed):
            block = jnp.broadcast_to(value[i:i + 1, :], (LANES, LANES))
            ref[i * LANES:(i + 1) * LANES, :] = jnp.transpose(block)

    def row_pass(q):
        @pl.loop(0, blocks)
        def _(b):
            at_rows = pl.ds(pl.multiple_of(b * BLOCK, BLOCK), BLOCK)
            acc = racc[at_rows, :] if q else None
            for j in range(part // LANES):
                at = pl.ds(q * part + j * LANES, LANES)
                term = table[at_rows, at].astype(F32) * colv[:, at]
                acc = term if acc is None else acc + term
            racc[at_rows, :] = acc

    def col_pass(q):
        acc8[:, pl.ds(q * part, part)] = jnp.zeros((8, part), F32)

        @pl.loop(0, blocks)
        def _(b):
            at_rows = pl.ds(pl.multiple_of(b * BLOCK, BLOCK), BLOCK)
            by_row = rscale[at_rows, :]
            for j in range(part // LANES):
                at = pl.ds(q * part + j * LANES, LANES)
                term = table[at_rows, at].astype(F32) * by_row
                acc8[:, at] += jnp.sum(term.reshape(BLOCK // 8, 8, LANES), axis=0)

    def row_exchange_start(sweep):
        for _, k, xx, yy, cc in group:
            pltpu.make_async_remote_copy(
                src_ref=rmsg[sweep],
                dst_ref=rbuf[sweep].at[k - 1],
                send_sem=row_send.at[sweep],
                recv_sem=row_recv.at[sweep],
                device_id=place(xx, z, yy, cc),
                device_id_type=MESH,
            ).start()

    def row_exchange_end(sweep):
        bulk_wait(rbuf[sweep], row_recv.at[sweep])
        return rmsg[sweep][...] + jnp.sum(rbuf[sweep][...], axis=0)

    def scale_probs():
        @pl.loop(0, blocks)
        def _(b):
            at_rows = pl.ds(pl.multiple_of(b * BLOCK, BLOCK), BLOCK)
            by_row = sscale[at_rows, :]
            for j in range(cols // LANES):
                at = pl.ds(j * LANES, LANES)
                expo[at_rows, at] = expo[at_rows, at] * by_row

    for sweep in range(SWEEPS):
        if sweep > 0:
            for q in range(PARTS):
                col_pass(q)
                col_send_part(sweep, q)
        if sweep == 1:
            student_arrived(x_order[-1])
            rmsg[sweep][sz.packed:, :] = pack(sacc)
        for q in range(PARTS):
            col_recv_part(sweep, q)
            row_pass(q)
        rmsg[sweep][0:sz.packed, :] = pack(racc)
        row_exchange_start(sweep)
        if sweep == 0:
            student_forward()
            for d in x_order[:-1]:
                student_arrived(d)
        if sweep == SWEEPS - 1:
            scale_probs()
        total = row_exchange_end(sweep)
        if sweep == 1:
            unpack((LOSS_SCALE / STUDENT_TEMP) / total[sz.packed:, :], sscale)
            total = total[0:sz.packed, :]
        if sweep == SWEEPS - 1:
            unpack((LOSS_SCALE / STUDENT_TEMP) / total, rscale)
        else:
            unpack(1.0 / total, rscale)

    def gradient_tile(t):
        at = pl.ds(t * tile, tile)

        @pl.loop(0, blocks)
        def _(b):
            at_rows = pl.ds(pl.multiple_of(b * BLOCK, BLOCK), BLOCK)
            by_row = rscale[at_rows, :]
            for j in range(chunks):
                at_j = pl.ds(t * tile + j * LANES, LANES)
                target = (table[at_rows, at_j].astype(F32) * by_row) * colv[:, at_j]
                table[at_rows, at_j] = (expo[at_rows, at_j] - target).astype(BF16)

        pg = jnp.dot(sht[...], table[:, at], preferred_element_type=F32)
        inv = winv[:, at]
        pu = wbuf[:, at].astype(F32) * inv
        dots = jnp.sum(pu * pg, axis=0, keepdims=True)
        out = (pg - pu * dots) * inv
        grad[:, :, :, at] = out.reshape(nx, nz, sz.bw, tile)

    def unit_tile(t):
        at = pl.ds(t * tile, tile)
        more = jnp.dot(table[:, at], pht[at, :], preferred_element_type=F32)
        unit[...] = more if t == 0 else unit[...] + more

    def ring_block(stream, s):
        if stream % 2 == 0:
            return (z + 2 * nz - 1 - s) % nz
        return (z + 1 + s) % nz

    def ring_send_copy(stream, s, src):
        return pltpu.make_async_remote_copy(
            src_ref=src,
            dst_ref=ring.at[stream, s],
            send_sem=ring_send.at[stream, s],
            recv_sem=ring_recv.at[stream, s],
            device_id=place(x, zs[1 if stream % 2 == 0 else nz - 1], y, c),
            device_id_type=MESH,
        )

    def begin(stream):
        block = grad.at[:, ring_block(stream, 0), :, pl.ds(stream * tile, tile)]
        ring_send_copy(stream, 0, block).start()

    def serve(stream, s, last=False):
        slot = ring.at[stream, s]
        bulk_wait(slot, ring_recv.at[stream, s])
        at = pl.ds(stream * tile, tile)
        slot[...] = slot[...] + grad[:, ring_block(stream, s + 1), :, at]
        if not last:
            ring_send_copy(stream, s + 1, slot).start()

    def out_slice(stream):
        return gw_ref.at[:, pl.ds(pl.multiple_of(x * cols + stream * tile, tile), tile)]

    def own_copy(stream):
        return pltpu.make_async_copy(
            ring.at[stream, sz.steps - 1, x], out_slice(stream), own_sem.at[stream]
        )

    def deliver(stream):
        for d in range(1, nx):
            pltpu.make_async_remote_copy(
                src_ref=ring.at[stream, sz.steps - 1, xs[d]],
                dst_ref=out_slice(stream),
                send_sem=x_send.at[stream, d - 1],
                recv_sem=x_recv.at[stream, d - 1],
                device_id=place(xs[d], z, y, c),
                device_id_type=MESH,
            ).start()
        own_copy(stream).start()

    early = range(0, TILES // 2)
    late = range(TILES // 2, TILES)
    for t in range(TILES):
        gradient_tile(t)
        begin(t)
        if t >= len(early) - 1:
            n = t + 1 - len(early)
            serve(n % len(early), n // len(early))
    after = [(late[0], 0)]
    for stream in early[1:]:
        after += [(stream, 1), (len(early) + stream, 0)]
    for t in range(TILES):
        unit_tile(t)
        if t < len(after):
            serve(*after[t])

    def unit_send(entry):
        _, k, xx, yy, cc = entry
        first = xx * rows + (yy * nc + cc) * sz.share
        pltpu.make_async_remote_copy(
            src_ref=unit.at[pl.ds(pl.multiple_of(first, sz.share), sz.share)],
            dst_ref=ubuf.at[k - 1],
            send_sem=u_send,
            recv_sem=u_recv,
            device_id=place(xx, z, yy, cc),
            device_id_type=MESH,
        ).start()

    def ring_steps(first, last):
        @pl.loop(first, last)
        def _(s):
            for stream in late:
                serve(stream, s)
            for stream in early:
                serve(stream, s + 1)

    spaced = max(min(3, sz.steps - 2), 1)
    waiting = list(group)
    slots = (spaced - 1) * TILES
    for n in range(slots):
        s, i = 1 + n // TILES, n % TILES
        if i < len(late):
            serve(late[i], s)
        else:
            serve(early[i - len(late)], s + 1)
        for _ in range(-(-len(group) // slots)):
            if waiting:
                unit_send(waiting.pop(0))
    for entry in waiting:
        unit_send(entry)

    middle = max(sz.steps - 2, spaced)
    ring_steps(spaced, middle)

    mine = pl.ds(pl.multiple_of((y * nc + c) * sz.share, sz.share), sz.share)
    bulk_wait(ubuf, u_recv)
    first = pl.multiple_of(x * rows + (y * nc + c) * sz.share, sz.share)
    total = unit[pl.ds(first, sz.share), :]
    for k in range(sz.group - 1):
        total = total + ubuf[k]
    unit_mine = sbuf[x, mine]
    along = jnp.sum(unit_mine * total, axis=1, keepdims=True)
    rowg[mine, :] = (total - unit_mine * along) / snorm[mine, 0:1]
    for k in range(1, ny * nc):
        pltpu.make_async_remote_copy(
            src_ref=rowg.at[mine],
            dst_ref=rowg.at[mine],
            send_sem=g_send,
            recv_sem=g_recv,
            device_id=place(x, z, ys[k // nc], cs[k % nc]),
            device_id_type=MESH,
        ).start()

    ring_steps(middle, sz.steps - 2)
    for stream in late:
        serve(stream, sz.steps - 2)
    for stream in early:
        serve(stream, sz.steps - 1, last=True)
        deliver(stream)
    for stream in late:
        serve(stream, sz.steps - 1, last=True)
        deliver(stream)

    others = pl.ds(0, rows - sz.share)
    bulk_wait(rowg.at[others], g_recv)
    bulk_wait(rowg.at[others], g_send)
    for which, buf in ((0, tbuf), (1, sbuf)):
        for d in x_order:
            if which == 1 or d in near:
                spread(buf, which, d).wait_send()
            forward(buf, which, d).wait_send()
    if far:
        relay(0).wait_send()
        relay(1).wait_send()
    for sweep in range(SWEEPS):
        for q in range(PARTS):
            bulk_wait(colbuf.at[sweep, q], col_send.at[sweep, q])
        bulk_wait(rbuf[sweep], row_send.at[sweep])
    bulk_wait(ubuf, u_send)

    @pl.loop(0, sz.steps)
    def _(s):
        for stream in range(TILES):
            bulk_wait(ring.at[stream, s], ring_send.at[stream, s])

    for stream in range(TILES):
        own_copy(stream).wait()
        for d in range(1, nx):
            bulk_wait(ring.at[stream, 0, 0], x_send.at[stream, d - 1])
            bulk_wait(ring.at[stream, 0, 0], x_recv.at[stream, d - 1])


def finish(sz, mask_ref, rowg_ref, gw_in, gs_ref, gw_out):
    gw_out[...] = gw_in[...]
    at = lax.broadcasted_iota(jnp.int32, (sz.patches, sz.rows), 0)
    picks = jnp.where(at == mask_ref[...], 1.0, 0.0).astype(BF16)
    rest = rowg_ref[...]
    out = None
    for _ in range(3):
        piece = rest.astype(BF16)
        rest = rest - piece.astype(F32)
        term = jnp.dot(picks, piece, preferred_element_type=F32)
        out = term if out is None else out + term
    gs_ref[...] = out


def per_device(sz, student_patches, teacher_patches, weights_raw, masked_rows):
    vmem = pl.BlockSpec(memory_space=pltpu.VMEM)
    anywhere = pl.BlockSpec(memory_space=pl.ANY)
    dma = pltpu.SemaphoreType.DMA
    g = sz.group
    nx, nz = sz.nx, sz.nz
    p = sz.packed
    scratch = [
        pltpu.VMEM((sz.patches, sz.width), BF16),
        pltpu.VMEM((sz.patches, sz.width), BF16),
        pltpu.VMEM((sz.width, sz.cols), BF16),
        pltpu.VMEM((sz.width, sz.cols), BF16),
        pltpu.VMEM((sz.cols, sz.width), BF16),
        pltpu.VMEM((1, sz.cols), F32),
        pltpu.VMEM((nx, sz.rows, sz.width), F32),
        pltpu.VMEM((nx, sz.rows, sz.width), F32),
        pltpu.VMEM((sz.rows, LANES), F32),
        pltpu.VMEM((sz.width, sz.all_rows), BF16),
        pltpu.VMEM((sz.all_rows, sz.cols), BF16),
        pltpu.VMEM((sz.all_rows, sz.cols), F32),
        pltpu.VMEM((8, sz.cols), F32),
        pltpu.VMEM((1, sz.cols), F32),
        pltpu.VMEM((SWEEPS, PARTS, 1, sz.part), F32),
        pltpu.VMEM((SWEEPS, PARTS, nz - 1, 1, sz.part), F32),
        pltpu.VMEM((sz.all_rows, LANES), F32),
        pltpu.VMEM((sz.all_rows, LANES), F32),
        pltpu.VMEM((sz.all_rows, LANES), F32),
        pltpu.VMEM((sz.all_rows, LANES), F32),
        pltpu.VMEM((p, LANES), F32),
        pltpu.VMEM((2 * p, LANES), F32),
        pltpu.VMEM((p, LANES), F32),
        pltpu.VMEM((g - 1, p, LANES), F32),
        pltpu.VMEM((g - 1, 2 * p, LANES), F32),
        pltpu.VMEM((g - 1, p, LANES), F32),
        pltpu.VMEM((sz.all_rows, sz.width), F32),
        pltpu.VMEM((g - 1, sz.share, sz.width), F32),
        pltpu.VMEM((nx, nz, sz.bw, sz.cols), F32),
        pltpu.VMEM((TILES, sz.steps, nx, sz.bw, sz.tile), F32),
        dma((2,)),
        dma(()),
        dma((TILES,)),
        dma((2, nx - 1)),
        dma((2, nx - 1)),
        dma((2,)),
        dma((2,)),
        dma((2, nx - 1)),
        dma((2, nx - 1)),
        dma((SWEEPS, PARTS)),
        dma((SWEEPS, PARTS)),
        dma((SWEEPS,)),
        dma((SWEEPS,)),
        dma(()),
        dma(()),
        dma(()),
        dma(()),
        dma((TILES, sz.steps)),
        dma((TILES, sz.steps)),
        dma((TILES, nx - 1)),
        dma((TILES, nx - 1)),
    ]
    picked = masked_rows.reshape(1, sz.rows)
    row_grad, grad_weight = pl.pallas_call(
        functools.partial(kernel, sz),
        out_shape=(
            jax.ShapeDtypeStruct((sz.rows, sz.width), F32),
            jax.ShapeDtypeStruct((sz.bw, sz.cols_dp), F32),
        ),
        in_specs=[vmem, anywhere, anywhere, anywhere],
        out_specs=(vmem, anywhere),
        scratch_shapes=scratch,
        compiler_params=pltpu.CompilerParams(
            collective_id=0, has_side_effects=True, vmem_limit_bytes=56 * 1024 * 1024
        ),
        cost_estimate=pl.CostEstimate(
            flops=8 * sz.all_rows * sz.cols * sz.width,
            bytes_accessed=4 * sz.width * sz.cols,
            transcendentals=2 * sz.all_rows * sz.cols,
        ),
        name="sinkhorn_loss",
    )(picked, student_patches, teacher_patches, weights_raw)
    return pl.pallas_call(
        functools.partial(finish, sz),
        out_shape=(
            jax.ShapeDtypeStruct((sz.patches, sz.width), F32),
            jax.ShapeDtypeStruct((sz.bw, sz.cols_dp), F32),
        ),
        in_specs=[vmem, vmem, vmem],
        out_specs=(vmem, vmem),
        name="finish",
    )(picked, row_grad, grad_weight)


def solution(mesh):
    placed = (P("dp", None), P("dp", None), P(None, "proto"), P("dp"))
    mesh_shape = (mesh.shape["dp"], mesh.shape["proto"])

    def body(student_patches, teacher_patches, weights_raw, masked_rows):
        sz = Sizes(
            mesh_shape,
            weights_raw.shape[0],
            student_patches.shape[0],
            masked_rows.shape[0],
            weights_raw.shape[1],
        )
        return per_device(sz, student_patches, teacher_patches, weights_raw, masked_rows)

    return jax.shard_map(
        body,
        mesh=mesh,
        in_specs=placed,
        out_specs=(P("dp", None), P("dp", "proto")),
        check_vma=False,
    )
```

```python
import functools
import math

import jax
import jax.numpy as jnp
from jax import lax
from jax.experimental import pallas as pl
from jax.experimental.pallas import tpu as pltpu
from jax.sharding import PartitionSpec as P

MESH = pl.DeviceIdType.MESH
F32 = jnp.float32
BF16 = jnp.bfloat16
SWEEPS = 3
TEACHER_TEMP = 0.07
STUDENT_TEMP = 0.1
LOSS_SCALE = 2048.0
LOG2E = math.log2(math.e)
LANES = 128
TILES = 8
PARTS = 4
BLOCK = 128


class Sizes:
    def __init__(self, mesh_shape, width, patches, rows, protos):
        n_dp, n_proto = mesh_shape
        self.nc = 2
        self.ny = n_proto // 2
        self.nx = 4 if n_dp >= 16 else 2
        self.nz = n_dp // self.nx
        self.width = width
        self.patches = patches
        self.rows = rows
        self.all_rows = rows * self.nx
        self.cols_dp = protos
        self.cols = protos // self.nx
        self.tile = self.cols // TILES
        self.part = self.cols // PARTS
        self.bw = width // n_dp
        self.group = self.nx * self.ny * self.nc
        self.packed = self.all_rows // LANES
        self.share = rows // (self.ny * self.nc)
        self.steps = self.nz - 1


def bulk_wait(ref, sem):
    pltpu.make_async_copy(ref, ref, sem).wait()


def ring_distance(step, size):
    return min(step, size - step)


def kernel(
    sz, mask_ref, stu_hbm, tea_hbm, w_hbm, gs_ref, gw_ref,
    stu_ref, tea_ref, wbuf, ph, pht, winv, tbuf, sbuf, snorm, sht, table, expo,
    acc8, colv, colmsg, colbuf, racc, sacc, rscale, sscale,
    rmsg0, rmsg1, rmsg2, rbuf0, rbuf1, rbuf2,
    unit, ubuf, grad, ring, rowg,
    in_sem, w_sem, own_sem, ts_send, ts_recv, rl_send, rl_recv, fw_send, fw_recv,
    col_send, col_recv,
    row_send, row_recv, u_send, u_recv, g_send, g_recv, ring_send, ring_recv, x_send, x_recv,
):
    nx, ny, nc, nz = sz.nx, sz.ny, sz.nc, sz.nz
    rows, cols, tile, part = sz.rows, sz.cols, sz.tile, sz.part
    chunks = tile // LANES
    blocks = sz.all_rows // BLOCK
    rmsg = (rmsg0, rmsg1, rmsg2)
    rbuf = (rbuf0, rbuf1, rbuf2)
    dp = lax.axis_index("dp")
    pr = lax.axis_index("proto")
    x, z = dp // nz, dp % nz
    y, c = pr // nc, pr % nc
    half = rows // nc

    xs = [x] + [(x + d) % nx for d in range(1, nx)]
    ys = [y] + [(y + d) % ny for d in range(1, ny)]
    cs = [c] + [(c + d) % nc for d in range(1, nc)]
    zs = [z] + [(z + d) % nz for d in range(1, nz)]

    def place(xx, zz, yy, cc):
        return (xx * nz + zz, yy * nc + cc)

    group = []
    for k in range(1, sz.group):
        dx, dy, dc = k // (ny * nc), (k // nc) % ny, k % nc
        far = ring_distance(dx, nx) + ring_distance(dy, ny)
        group.append((-far, k, xs[dx], ys[dy], cs[dc]))
    group.sort(key=lambda entry: entry[:2])
    z_order = sorted(range(1, nz), key=lambda d: -ring_distance(d, nz))

    barrier = pltpu.get_barrier_semaphore()
    for _, _, xx, yy, cc in group:
        pl.semaphore_signal(barrier, inc=1, device_id=place(xx, z, yy, cc), device_id_type=MESH)
    for d in z_order:
        pl.semaphore_signal(barrier, inc=1, device_id=place(x, zs[d], y, c), device_id_type=MESH)

    tea_copy = pltpu.make_async_copy(tea_hbm, tea_ref, in_sem.at[0])
    stu_copy = pltpu.make_async_copy(stu_hbm, stu_ref, in_sem.at[1])
    w_copy = pltpu.make_async_copy(
        w_hbm.at[:, pl.ds(pl.multiple_of(x * cols, cols), cols)], wbuf, w_sem
    )
    tea_copy.start()
    stu_copy.start()
    w_copy.start()

    def one_hot():
        at = lax.broadcasted_iota(jnp.int32, (sz.patches, rows), 0)
        return jnp.where(at == mask_ref[...], 1.0, 0.0).astype(BF16)

    one_hot_t = one_hot()

    def unit_rows(ref):
        picked = lax.dot_general(
            one_hot_t, ref[...], (((0,), (0,)), ((), ())), preferred_element_type=F32
        )
        norm = jnp.sqrt(jnp.sum(picked * picked, axis=1, keepdims=True) + 1e-06)
        return picked / norm, norm

    tea_copy.wait()
    tbuf[x] = unit_rows(tea_ref)[0]
    stu_copy.wait()
    stu_unit, stu_norm = unit_rows(stu_ref)
    sbuf[x] = stu_unit
    snorm[...] = jnp.broadcast_to(stu_norm, (rows, LANES))

    pl.semaphore_wait(barrier, sz.group - 1 + nz - 1)

    my_half = pl.ds(pl.multiple_of(c * half, half), half)

    def spread(buf, which, d):
        return pltpu.make_async_remote_copy(
            src_ref=buf.at[x, my_half],
            dst_ref=buf.at[x, my_half],
            send_sem=ts_send.at[which, d - 1],
            recv_sem=ts_recv.at[which, d - 1],
            device_id=place(xs[d], z, y, c),
            device_id_type=MESH,
        )

    def forward(buf, which, d):
        return pltpu.make_async_remote_copy(
            src_ref=buf.at[xs[nx - d], my_half],
            dst_ref=buf.at[xs[nx - d], my_half],
            send_sem=fw_send.at[which, d - 1],
            recv_sem=fw_recv.at[which, d - 1],
            device_id=place(x, z, y, cs[1]),
            device_id_type=MESH,
        )

    x_order = sorted(range(1, nx), key=lambda d: ring_distance(d, nx))
    for d in x_order[:2]:
        spread(tbuf, 0, d).start()

    w_copy.wait()
    for t in range(TILES):
        at = pl.ds(t * tile, tile)
        w = wbuf[:, at].astype(F32)
        inv = 1.0 / jnp.sqrt(jnp.sum(w * w, axis=0, keepdims=True) + 1e-06)
        winv[:, at] = inv
        proto = (w * inv).astype(BF16)
        ph[:, at] = proto
        pht[at, :] = jnp.transpose(proto)

    def col_send_part(sweep, q):
        at = pl.ds(q * part, part)
        colmsg[sweep, q] = jnp.sum(acc8[:, at], axis=0, keepdims=True)
        for d in z_order:
            pltpu.make_async_remote_copy(
                src_ref=colmsg.at[sweep, q],
                dst_ref=colbuf.at[sweep, q, d - 1],
                send_sem=col_send.at[sweep, q],
                recv_sem=col_recv.at[sweep, q],
                device_id=place(x, zs[d], y, c),
                device_id_type=MESH,
            ).start()

    def col_recv_part(sweep, q):
        bulk_wait(colbuf.at[sweep, q], col_recv.at[sweep, q])
        total = colmsg[sweep, q]
        for k in range(nz - 1):
            total = total + colbuf[sweep, q, k]
        colv[:, pl.ds(q * part, part)] = 1.0 / total

    def teacher_block(xb, first=False, last=False):
        half_rows = tbuf[xb].astype(BF16)
        at_rows = pl.ds(pl.multiple_of(xb * rows, rows), rows)
        for t in range(TILES):
            at = pl.ds(t * tile, tile)
            dots = jnp.dot(half_rows, ph[:, at], preferred_element_type=F32)
            entry = jnp.exp2(dots * (LOG2E / TEACHER_TEMP)).astype(BF16)
            table[at_rows, at] = entry
            total = jnp.sum(entry.astype(F32).reshape(rows // 8, 8, tile), axis=0)
            acc8[:, at] = total if first else acc8[:, at] + total
            if last and (t + 1) % (TILES // PARTS) == 0:
                col_send_part(0, t // (TILES // PARTS))

    def student_block(xb):
        half_rows = sbuf[xb].astype(BF16)
        at_rows = pl.ds(pl.multiple_of(xb * rows, rows), rows)
        sht[:, at_rows] = jnp.transpose(sbuf[xb]).astype(BF16)
        wide = cols // 2
        total = None
        for t in range(2):
            at = pl.ds(t * wide, wide)
            dots = jnp.dot(half_rows, ph[:, at], preferred_element_type=F32)
            ex = jnp.exp2(dots * (LOG2E / STUDENT_TEMP))
            expo[at_rows, at] = ex
            for i in range(wide // LANES):
                piece = ex[:, i * LANES:(i + 1) * LANES]
                total = piece if total is None else total + piece
        sacc[at_rows, :] = total

    def half_arrived(buf, which, d):
        one = buf.at[0, pl.ds(0, half)]
        pltpu.make_async_copy(one, one, fw_recv.at[which, d - 1]).wait()

    quarter = half // 2

    def relay(n):
        block = xs[nx - 1] if n == 0 else xs[1]
        piece = tbuf.at[block, pl.ds(pl.multiple_of(c * half + n * quarter, quarter), quarter)]
        return pltpu.make_async_remote_copy(
            src_ref=piece,
            dst_ref=piece,
            send_sem=rl_send.at[n],
            recv_sem=rl_recv.at[n],
            device_id=place(xs[1] if n == 0 else xs[nx - 1], z, y, c),
            device_id_type=MESH,
        )

    near = x_order[:2]
    far = x_order[2:]
    teacher_block(x, first=True)
    for n, d in enumerate(near):
        spread(tbuf, 0, d).wait_recv()
        if far:
            relay(n).start()
        forward(tbuf, 0, d).start()
    student_block(x)
    for d in near:
        half_arrived(tbuf, 0, d)
        teacher_block(xs[nx - d], last=d == x_order[-1])
    if far:
        relay(0).wait_recv()
        relay(1).wait_recv()
        forward(tbuf, 0, far[0]).start()
    for d in x_order:
        spread(sbuf, 1, d).start()
    for d in far:
        half_arrived(tbuf, 0, d)
        teacher_block(xs[nx - d], last=True)

    def student_forward():
        for d in x_order:
            spread(sbuf, 1, d).wait_recv()
            forward(sbuf, 1, d).start()

    def student_arrived(d):
        half_arrived(sbuf, 1, d)
        student_block(xs[nx - d])

    def pack(ref):
        parts = []
        for i in range(sz.packed):
            block = ref[i * LANES:(i + 1) * LANES, :]
            parts.append(jnp.sum(jnp.transpose(block), axis=0, keepdims=True))
        return jnp.concatenate(parts, axis=0)

    def unpack(value, ref):
        for i in range(sz.packed):
            block = jnp.broadcast_to(value[i:i + 1, :], (LANES, LANES))
            ref[i * LANES:(i + 1) * LANES, :] = jnp.transpose(block)

    def row_pass(q):
        @pl.loop(0, blocks)
        def _(b):
            at_rows = pl.ds(pl.multiple_of(b * BLOCK, BLOCK), BLOCK)
            acc = racc[at_rows, :] if q else None
            for j in range(part // LANES):
                at = pl.ds(q * part + j * LANES, LANES)
                term = table[at_rows, at].astype(F32) * colv[:, at]
                acc = term if acc is None else acc + term
            racc[at_rows, :] = acc

    def col_pass(q):
        acc8[:, pl.ds(q * part, part)] = jnp.zeros((8, part), F32)

        @pl.loop(0, blocks)
        def _(b):
            at_rows = pl.ds(pl.multiple_of(b * BLOCK, BLOCK), BLOCK)
            by_row = rscale[at_rows, :]
            for j in range(part // LANES):
                at = pl.ds(q * part + j * LANES, LANES)
                term = table[at_rows, at].astype(F32) * by_row
                acc8[:, at] += jnp.sum(term.reshape(BLOCK // 8, 8, LANES), axis=0)

    def row_exchange_start(sweep):
        for _, k, xx, yy, cc in group:
            pltpu.make_async_remote_copy(
                src_ref=rmsg[sweep],
                dst_ref=rbuf[sweep].at[k - 1],
                send_sem=row_send.at[sweep],
                recv_sem=row_recv.at[sweep],
                device_id=place(xx, z, yy, cc),
                device_id_type=MESH,
            ).start()

    def row_exchange_end(sweep):
        bulk_wait(rbuf[sweep], row_recv.at[sweep])
        return rmsg[sweep][...] + jnp.sum(rbuf[sweep][...], axis=0)

    def scale_probs():
        @pl.loop(0, blocks)
        def _(b):
            at_rows = pl.ds(pl.multiple_of(b * BLOCK, BLOCK), BLOCK)
            by_row = sscale[at_rows, :]
            for j in range(cols // LANES):
                at = pl.ds(j * LANES, LANES)
                expo[at_rows, at] = expo[at_rows, at] * by_row

    for sweep in range(SWEEPS):
        if sweep > 0:
            for q in range(PARTS):
                col_pass(q)
                col_send_part(sweep, q)
        if sweep == 1:
            student_arrived(x_order[-1])
            rmsg[sweep][sz.packed:, :] = pack(sacc)
        for q in range(PARTS):
            col_recv_part(sweep, q)
            row_pass(q)
        rmsg[sweep][0:sz.packed, :] = pack(racc)
        row_exchange_start(sweep)
        if sweep == 0:
            student_forward()
            for d in x_order[:-1]:
                student_arrived(d)
        if sweep == SWEEPS - 1:
            scale_probs()
        total = row_exchange_end(sweep)
        if sweep == 1:
            unpack((LOSS_SCALE / STUDENT_TEMP) / total[sz.packed:, :], sscale)
            total = total[0:sz.packed, :]
        if sweep == SWEEPS - 1:
            unpack((LOSS_SCALE / STUDENT_TEMP) / total, rscale)
        else:
            unpack(1.0 / total, rscale)

    def gradient_tile(t):
        at = pl.ds(t * tile, tile)

        @pl.loop(0, blocks)
        def _(b):
            at_rows = pl.ds(pl.multiple_of(b * BLOCK, BLOCK), BLOCK)
            by_row = rscale[at_rows, :]
            for j in range(chunks):
                at_j = pl.ds(t * tile + j * LANES, LANES)
                target = (table[at_rows, at_j].astype(F32) * by_row) * colv[:, at_j]
                table[at_rows, at_j] = (expo[at_rows, at_j] - target).astype(BF16)

        pg = jnp.dot(sht[...], table[:, at], preferred_element_type=F32)
        inv = winv[:, at]
        pu = wbuf[:, at].astype(F32) * inv
        dots = jnp.sum(pu * pg, axis=0, keepdims=True)
        out = (pg - pu * dots) * inv
        grad[:, :, :, at] = out.reshape(nx, nz, sz.bw, tile)

    def unit_tile(t):
        at = pl.ds(t * tile, tile)
        more = jnp.dot(table[:, at], pht[at, :], preferred_element_type=F32)
        unit[...] = more if t == 0 else unit[...] + more

    def ring_block(stream, s):
        if stream % 2 == 0:
            return (z + 2 * nz - 1 - s) % nz
        return (z + 1 + s) % nz

    def ring_send_copy(stream, s, src):
        return pltpu.make_async_remote_copy(
            src_ref=src,
            dst_ref=ring.at[stream, s],
            send_sem=ring_send.at[stream, s],
            recv_sem=ring_recv.at[stream, s],
            device_id=place(x, zs[1 if stream % 2 == 0 else nz - 1], y, c),
            device_id_type=MESH,
        )

    def begin(stream):
        block = grad.at[:, ring_block(stream, 0), :, pl.ds(stream * tile, tile)]
        ring_send_copy(stream, 0, block).start()

    def serve(stream, s, last=False):
        slot = ring.at[stream, s]
        bulk_wait(slot, ring_recv.at[stream, s])
        at = pl.ds(stream * tile, tile)
        slot[...] = slot[...] + grad[:, ring_block(stream, s + 1), :, at]
        if not last:
            ring_send_copy(stream, s + 1, slot).start()

    def out_slice(stream):
        return gw_ref.at[:, pl.ds(pl.multiple_of(x * cols + stream * tile, tile), tile)]

    def own_copy(stream):
        return pltpu.make_async_copy(
            ring.at[stream, sz.steps - 1, x], out_slice(stream), own_sem.at[stream]
        )

    def deliver(stream):
        for d in reversed(x_order):
            pltpu.make_async_remote_copy(
                src_ref=ring.at[stream, sz.steps - 1, xs[d]],
                dst_ref=out_slice(stream),
                send_sem=x_send.at[stream, d - 1],
                recv_sem=x_recv.at[stream, d - 1],
                device_id=place(xs[d], z, y, c),
                device_id_type=MESH,
            ).start()
        own_copy(stream).start()

    early = range(0, TILES // 2)
    late = range(TILES // 2, TILES)
    for t in range(TILES):
        gradient_tile(t)
        begin(t)
        if t >= len(early) - 1:
            n = t + 1 - len(early)
            serve(n % len(early), n // len(early))
    after = [(late[0], 0)]
    for stream in early[1:]:
        after += [(stream, 1), (len(early) + stream, 0)]
    for t in range(TILES):
        unit_tile(t)
        if t < len(after):
            serve(*after[t])

    def unit_send(entry):
        _, k, xx, yy, cc = entry
        first = xx * rows + (yy * nc + cc) * sz.share
        pltpu.make_async_remote_copy(
            src_ref=unit.at[pl.ds(pl.multiple_of(first, sz.share), sz.share)],
            dst_ref=ubuf.at[k - 1],
            send_sem=u_send,
            recv_sem=u_recv,
            device_id=place(xx, z, yy, cc),
            device_id_type=MESH,
        ).start()

    def ring_steps(first, last):
        @pl.loop(first, last)
        def _(s):
            for stream in late:
                serve(stream, s)
            for stream in early:
                serve(stream, s + 1)

    spaced = max(min(3, sz.steps - 2), 1)
    waiting = list(group)
    slots = (spaced - 1) * TILES
    for n in range(slots):
        s, i = 1 + n // TILES, n % TILES
        if i < len(late):
            serve(late[i], s)
        else:
            serve(early[i - len(late)], s + 1)
        for _ in range(-(-len(group) // slots)):
            if waiting:
                unit_send(waiting.pop(0))
    for entry in waiting:
        unit_send(entry)

    middle = max(sz.steps - 2, spaced)
    ring_steps(spaced, middle)

    mine = pl.ds(pl.multiple_of((y * nc + c) * sz.share, sz.share), sz.share)
    bulk_wait(ubuf, u_recv)
    first = pl.multiple_of(x * rows + (y * nc + c) * sz.share, sz.share)
    total = unit[pl.ds(first, sz.share), :]
    for k in range(sz.group - 1):
        total = total + ubuf[k]
    unit_mine = sbuf[x, mine]
    along = jnp.sum(unit_mine * total, axis=1, keepdims=True)
    rowg[mine, :] = (total - unit_mine * along) / snorm[mine, 0:1]
    for k in range(1, ny * nc):
        pltpu.make_async_remote_copy(
            src_ref=rowg.at[mine],
            dst_ref=rowg.at[mine],
            send_sem=g_send,
            recv_sem=g_recv,
            device_id=place(x, z, ys[k // nc], cs[k % nc]),
            device_id_type=MESH,
        ).start()

    ring_steps(middle, sz.steps - 2)
    for stream in late:
        serve(stream, sz.steps - 2)
    for stream in early:
        serve(stream, sz.steps - 1, last=True)
        deliver(stream)

    others = pl.ds(0, rows - sz.share)
    bulk_wait(rowg.at[others], g_recv)
    picks = one_hot()
    rest = rowg[...]
    out = None
    for _ in range(3):
        piece = rest.astype(BF16)
        rest = rest - piece.astype(F32)
        term = jnp.dot(picks, piece, preferred_element_type=F32)
        out = term if out is None else out + term
    gs_ref[...] = out

    for stream in late:
        serve(stream, sz.steps - 1, last=True)
        deliver(stream)

    bulk_wait(rowg.at[others], g_send)
    for which, buf in ((0, tbuf), (1, sbuf)):
        for d in x_order:
            if which == 1 or d in near:
                spread(buf, which, d).wait_send()
            forward(buf, which, d).wait_send()
    if far:
        relay(0).wait_send()
        relay(1).wait_send()
    for sweep in range(SWEEPS):
        for q in range(PARTS):
            bulk_wait(colbuf.at[sweep, q], col_send.at[sweep, q])
        bulk_wait(rbuf[sweep], row_send.at[sweep])
    bulk_wait(ubuf, u_send)

    @pl.loop(0, sz.steps)
    def _(s):
        for stream in range(TILES):
            bulk_wait(ring.at[stream, s], ring_send.at[stream, s])

    for stream in range(TILES):
        own_copy(stream).wait()
        for d in range(1, nx):
            bulk_wait(ring.at[stream, 0, 0], x_send.at[stream, d - 1])
            bulk_wait(ring.at[stream, 0, 0], x_recv.at[stream, d - 1])


def finish(gs_in, gw_in, gs_out, gw_out):
    gs_out[...] = gs_in[...]
    gw_out[...] = gw_in[...]


def per_device(sz, student_patches, teacher_patches, weights_raw, masked_rows):
    vmem = pl.BlockSpec(memory_space=pltpu.VMEM)
    anywhere = pl.BlockSpec(memory_space=pl.ANY)
    dma = pltpu.SemaphoreType.DMA
    g = sz.group
    nx, nz = sz.nx, sz.nz
    p = sz.packed
    scratch = [
        pltpu.VMEM((sz.patches, sz.width), BF16),
        pltpu.VMEM((sz.patches, sz.width), BF16),
        pltpu.VMEM((sz.width, sz.cols), BF16),
        pltpu.VMEM((sz.width, sz.cols), BF16),
        pltpu.VMEM((sz.cols, sz.width), BF16),
        pltpu.VMEM((1, sz.cols), F32),
        pltpu.VMEM((nx, sz.rows, sz.width), F32),
        pltpu.VMEM((nx, sz.rows, sz.width), F32),
        pltpu.VMEM((sz.rows, LANES), F32),
        pltpu.VMEM((sz.width, sz.all_rows), BF16),
        pltpu.VMEM((sz.all_rows, sz.cols), BF16),
        pltpu.VMEM((sz.all_rows, sz.cols), F32),
        pltpu.VMEM((8, sz.cols), F32),
        pltpu.VMEM((1, sz.cols), F32),
        pltpu.VMEM((SWEEPS, PARTS, 1, sz.part), F32),
        pltpu.VMEM((SWEEPS, PARTS, nz - 1, 1, sz.part), F32),
        pltpu.VMEM((sz.all_rows, LANES), F32),
        pltpu.VMEM((sz.all_rows, LANES), F32),
        pltpu.VMEM((sz.all_rows, LANES), F32),
        pltpu.VMEM((sz.all_rows, LANES), F32),
        pltpu.VMEM((p, LANES), F32),
        pltpu.VMEM((2 * p, LANES), F32),
        pltpu.VMEM((p, LANES), F32),
        pltpu.VMEM((g - 1, p, LANES), F32),
        pltpu.VMEM((g - 1, 2 * p, LANES), F32),
        pltpu.VMEM((g - 1, p, LANES), F32),
        pltpu.VMEM((sz.all_rows, sz.width), F32),
        pltpu.VMEM((g - 1, sz.share, sz.width), F32),
        pltpu.VMEM((nx, nz, sz.bw, sz.cols), F32),
        pltpu.VMEM((TILES, sz.steps, nx, sz.bw, sz.tile), F32),
        pltpu.VMEM((sz.rows, sz.width), F32),
        dma((2,)),
        dma(()),
        dma((TILES,)),
        dma((2, nx - 1)),
        dma((2, nx - 1)),
        dma((2,)),
        dma((2,)),
        dma((2, nx - 1)),
        dma((2, nx - 1)),
        dma((SWEEPS, PARTS)),
        dma((SWEEPS, PARTS)),
        dma((SWEEPS,)),
        dma((SWEEPS,)),
        dma(()),
        dma(()),
        dma(()),
        dma(()),
        dma((TILES, sz.steps)),
        dma((TILES, sz.steps)),
        dma((TILES, nx - 1)),
        dma((TILES, nx - 1)),
    ]
    picked = masked_rows.reshape(1, sz.rows)
    grad_student, grad_weight = pl.pallas_call(
        functools.partial(kernel, sz),
        out_shape=(
            jax.ShapeDtypeStruct((sz.patches, sz.width), F32),
            jax.ShapeDtypeStruct((sz.bw, sz.cols_dp), F32),
        ),
        in_specs=[vmem, anywhere, anywhere, anywhere],
        out_specs=(vmem, anywhere),
        scratch_shapes=scratch,
        compiler_params=pltpu.CompilerParams(
            collective_id=0, has_side_effects=True, vmem_limit_bytes=56 * 1024 * 1024
        ),
        cost_estimate=pl.CostEstimate(
            flops=8 * sz.all_rows * sz.cols * sz.width,
            bytes_accessed=4 * sz.width * sz.cols,
            transcendentals=2 * sz.all_rows * sz.cols,
        ),
        name="sinkhorn_loss",
    )(picked, student_patches, teacher_patches, weights_raw)
    return pl.pallas_call(
        finish,
        out_shape=(
            jax.ShapeDtypeStruct((sz.patches, sz.width), F32),
            jax.ShapeDtypeStruct((sz.bw, sz.cols_dp), F32),
        ),
        in_specs=[vmem, vmem],
        out_specs=(vmem, vmem),
        name="finish",
    )(grad_student, grad_weight)


def solution(mesh):
    placed = (P("dp", None), P("dp", None), P(None, "proto"), P("dp"))
    mesh_shape = (mesh.shape["dp"], mesh.shape["proto"])

    def body(student_patches, teacher_patches, weights_raw, masked_rows):
        sz = Sizes(
            mesh_shape,
            weights_raw.shape[0],
            student_patches.shape[0],
            masked_rows.shape[0],
            weights_raw.shape[1],
        )
        return per_device(sz, student_patches, teacher_patches, weights_raw, masked_rows)

    return jax.shard_map(
        body,
        mesh=mesh,
        in_specs=placed,
        out_specs=(P("dp", None), P("dp", "proto")),
        check_vma=False,
    )
```

```python
import functools
import math

import jax
import jax.numpy as jnp
from jax import lax
from jax.experimental import pallas as pl
from jax.experimental.pallas import tpu as pltpu
from jax.sharding import PartitionSpec as P

MESH = pl.DeviceIdType.MESH
F32 = jnp.float32
BF16 = jnp.bfloat16
SWEEPS = 3
TEACHER_TEMP = 0.07
STUDENT_TEMP = 0.1
LOSS_SCALE = 2048.0
LOG2E = math.log2(math.e)
LANES = 128
TILES = 8
PARTS = 4
BLOCK = 128


class Sizes:
    def __init__(self, mesh_shape, width, patches, rows, protos):
        n_dp, n_proto = mesh_shape
        self.nc = 2
        self.ny = n_proto // 2
        self.nx = 4 if n_dp >= 16 else 2
        self.nz = n_dp // self.nx
        self.width = width
        self.patches = patches
        self.rows = rows
        self.all_rows = rows * self.nx
        self.cols_dp = protos
        self.cols = protos // self.nx
        self.tile = self.cols // TILES
        self.part = self.cols // PARTS
        self.bw = width // n_dp
        self.group = self.nx * self.ny * self.nc
        self.packed = self.all_rows // LANES
        self.share = rows // (self.ny * self.nc)
        self.steps = self.nz - 1


def bulk_wait(ref, sem):
    pltpu.make_async_copy(ref, ref, sem).wait()


def ring_distance(step, size):
    return min(step, size - step)


def kernel(
    sz, mask_ref, stu_hbm, tea_hbm, w_hbm, rowg, gw_ref,
    stu_ref, tea_ref, wbuf, ph, pht, winv, tbuf, sbuf, snorm, sht, table, expo,
    acc8, colv, colmsg, colbuf, racc, sacc, rscale, sscale,
    rmsg0, rmsg1, rmsg2, rbuf0, rbuf1, rbuf2,
    unit, ubuf, grad, ring,
    in_sem, w_sem, own_sem, ts_send, ts_recv, rl_send, rl_recv, fw_send, fw_recv,
    col_send, col_recv,
    row_send, row_recv, u_send, u_recv, g_send, g_recv, ring_send, ring_recv, x_send, x_recv,
):
    nx, ny, nc, nz = sz.nx, sz.ny, sz.nc, sz.nz
    rows, cols, tile, part = sz.rows, sz.cols, sz.tile, sz.part
    chunks = tile // LANES
    blocks = sz.all_rows // BLOCK
    rmsg = (rmsg0, rmsg1, rmsg2)
    rbuf = (rbuf0, rbuf1, rbuf2)
    dp = lax.axis_index("dp")
    pr = lax.axis_index("proto")
    x, z = dp // nz, dp % nz
    y, c = pr // nc, pr % nc
    half = rows // nc

    xs = [x] + [(x + d) % nx for d in range(1, nx)]
    ys = [y] + [(y + d) % ny for d in range(1, ny)]
    cs = [c] + [(c + d) % nc for d in range(1, nc)]
    zs = [z] + [(z + d) % nz for d in range(1, nz)]

    def place(xx, zz, yy, cc):
        return (xx * nz + zz, yy * nc + cc)

    group = []
    for k in range(1, sz.group):
        dx, dy, dc = k // (ny * nc), (k // nc) % ny, k % nc
        far = ring_distance(dx, nx) + ring_distance(dy, ny)
        group.append((-far, k, xs[dx], ys[dy], cs[dc]))
    group.sort(key=lambda entry: entry[:2])
    z_order = sorted(range(1, nz), key=lambda d: -ring_distance(d, nz))

    barrier = pltpu.get_barrier_semaphore()
    for _, _, xx, yy, cc in group:
        pl.semaphore_signal(barrier, inc=1, device_id=place(xx, z, yy, cc), device_id_type=MESH)
    for d in z_order:
        pl.semaphore_signal(barrier, inc=1, device_id=place(x, zs[d], y, c), device_id_type=MESH)

    tea_copy = pltpu.make_async_copy(tea_hbm, tea_ref, in_sem.at[0])
    stu_copy = pltpu.make_async_copy(stu_hbm, stu_ref, in_sem.at[1])
    w_copy = pltpu.make_async_copy(
        w_hbm.at[:, pl.ds(pl.multiple_of(x * cols, cols), cols)], wbuf, w_sem
    )
    tea_copy.start()
    stu_copy.start()
    w_copy.start()

    at = lax.broadcasted_iota(jnp.int32, (sz.patches, rows), 0)
    one_hot_t = jnp.where(at == mask_ref[...], 1.0, 0.0).astype(BF16)

    def unit_rows(ref):
        picked = lax.dot_general(
            one_hot_t, ref[...], (((0,), (0,)), ((), ())), preferred_element_type=F32
        )
        norm = jnp.sqrt(jnp.sum(picked * picked, axis=1, keepdims=True) + 1e-06)
        return picked / norm, norm

    tea_copy.wait()
    tbuf[x] = unit_rows(tea_ref)[0]
    stu_copy.wait()
    stu_unit, stu_norm = unit_rows(stu_ref)
    sbuf[x] = stu_unit
    snorm[...] = jnp.broadcast_to(stu_norm, (rows, LANES))

    pl.semaphore_wait(barrier, sz.group - 1 + nz - 1)

    my_half = pl.ds(pl.multiple_of(c * half, half), half)

    def spread(buf, which, d):
        return pltpu.make_async_remote_copy(
            src_ref=buf.at[x, my_half],
            dst_ref=buf.at[x, my_half],
            send_sem=ts_send.at[which, d - 1],
            recv_sem=ts_recv.at[which, d - 1],
            device_id=place(xs[d], z, y, c),
            device_id_type=MESH,
        )

    def forward(buf, which, d):
        return pltpu.make_async_remote_copy(
            src_ref=buf.at[xs[nx - d], my_half],
            dst_ref=buf.at[xs[nx - d], my_half],
            send_sem=fw_send.at[which, d - 1],
            recv_sem=fw_recv.at[which, d - 1],
            device_id=place(x, z, y, cs[1]),
            device_id_type=MESH,
        )

    x_order = sorted(range(1, nx), key=lambda d: ring_distance(d, nx))
    for d in x_order[:2]:
        spread(tbuf, 0, d).start()

    w_copy.wait()
    for t in range(TILES):
        at = pl.ds(t * tile, tile)
        w = wbuf[:, at].astype(F32)
        inv = 1.0 / jnp.sqrt(jnp.sum(w * w, axis=0, keepdims=True) + 1e-06)
        winv[:, at] = inv
        proto = (w * inv).astype(BF16)
        ph[:, at] = proto
        pht[at, :] = jnp.transpose(proto)

    def col_send_part(sweep, q):
        at = pl.ds(q * part, part)
        colmsg[sweep, q] = jnp.sum(acc8[:, at], axis=0, keepdims=True)
        for d in z_order:
            pltpu.make_async_remote_copy(
                src_ref=colmsg.at[sweep, q],
                dst_ref=colbuf.at[sweep, q, d - 1],
                send_sem=col_send.at[sweep, q],
                recv_sem=col_recv.at[sweep, q],
                device_id=place(x, zs[d], y, c),
                device_id_type=MESH,
            ).start()

    def col_recv_part(sweep, q):
        bulk_wait(colbuf.at[sweep, q], col_recv.at[sweep, q])
        total = colmsg[sweep, q]
        for k in range(nz - 1):
            total = total + colbuf[sweep, q, k]
        colv[:, pl.ds(q * part, part)] = 1.0 / total

    def teacher_block(xb, first=False, last=False):
        half_rows = tbuf[xb].astype(BF16)
        at_rows = pl.ds(pl.multiple_of(xb * rows, rows), rows)
        for t in range(TILES):
            at = pl.ds(t * tile, tile)
            dots = jnp.dot(half_rows, ph[:, at], preferred_element_type=F32)
            entry = jnp.exp2(dots * (LOG2E / TEACHER_TEMP)).astype(BF16)
            table[at_rows, at] = entry
            total = jnp.sum(entry.astype(F32).reshape(rows // 8, 8, tile), axis=0)
            acc8[:, at] = total if first else acc8[:, at] + total
            if last and (t + 1) % (TILES // PARTS) == 0:
                col_send_part(0, t // (TILES // PARTS))

    def student_block(xb):
        half_rows = sbuf[xb].astype(BF16)
        at_rows = pl.ds(pl.multiple_of(xb * rows, rows), rows)
        sht[:, at_rows] = jnp.transpose(sbuf[xb]).astype(BF16)
        wide = cols // 2
        total = None
        for t in range(2):
            at = pl.ds(t * wide, wide)
            dots = jnp.dot(half_rows, ph[:, at], preferred_element_type=F32)
            ex = jnp.exp2(dots * (LOG2E / STUDENT_TEMP))
            expo[at_rows, at] = ex
            for i in range(wide // LANES):
                piece = ex[:, i * LANES:(i + 1) * LANES]
                total = piece if total is None else total + piece
        sacc[at_rows, :] = total

    def half_arrived(buf, which, d):
        one = buf.at[0, pl.ds(0, half)]
        pltpu.make_async_copy(one, one, fw_recv.at[which, d - 1]).wait()

    quarter = half // 2

    def relay(n):
        block = xs[nx - 1] if n == 0 else xs[1]
        piece = tbuf.at[block, pl.ds(pl.multiple_of(c * half + n * quarter, quarter), quarter)]
        return pltpu.make_async_remote_copy(
            src_ref=piece,
            dst_ref=piece,
            send_sem=rl_send.at[n],
            recv_sem=rl_recv.at[n],
            device_id=place(xs[1] if n == 0 else xs[nx - 1], z, y, c),
            device_id_type=MESH,
        )

    near = x_order[:2]
    far = x_order[2:]
    teacher_block(x, first=True)
    for n, d in enumerate(near):
        spread(tbuf, 0, d).wait_recv()
        if far:
            relay(n).start()
        forward(tbuf, 0, d).start()
    student_block(x)
    for d in near:
        half_arrived(tbuf, 0, d)
        teacher_block(xs[nx - d], last=d == x_order[-1])
    if far:
        relay(0).wait_recv()
        relay(1).wait_recv()
        forward(tbuf, 0, far[0]).start()
    for d in x_order:
        spread(sbuf, 1, d).start()
    for d in far:
        half_arrived(tbuf, 0, d)
        teacher_block(xs[nx - d], last=True)

    def student_forward():
        for d in x_order:
            spread(sbuf, 1, d).wait_recv()
            forward(sbuf, 1, d).start()

    def student_arrived(d):
        half_arrived(sbuf, 1, d)
        student_block(xs[nx - d])

    def pack(ref):
        parts = []
        for i in range(sz.packed):
            block = ref[i * LANES:(i + 1) * LANES, :]
            parts.append(jnp.sum(jnp.transpose(block), axis=0, keepdims=True))
        return jnp.concatenate(parts, axis=0)

    def unpack(value, ref):
        for i in range(sz.packed):
            block = jnp.broadcast_to(value[i:i + 1, :], (LANES, LANES))
            ref[i * LANES:(i + 1) * LANES, :] = jnp.transpose(block)

    def row_pass(q):
        @pl.loop(0, blocks)
        def _(b):
            at_rows = pl.ds(pl.multiple_of(b * BLOCK, BLOCK), BLOCK)
            acc = racc[at_rows, :] if q else None
            for j in range(part // LANES):
                at = pl.ds(q * part + j * LANES, LANES)
                term = table[at_rows, at].astype(F32) * colv[:, at]
                acc = term if acc is None else acc + term
            racc[at_rows, :] = acc

    def col_pass(q):
        acc8[:, pl.ds(q * part, part)] = jnp.zeros((8, part), F32)

        @pl.loop(0, blocks)
        def _(b):
            at_rows = pl.ds(pl.multiple_of(b * BLOCK, BLOCK), BLOCK)
            by_row = rscale[at_rows, :]
            for j in range(part // LANES):
                at = pl.ds(q * part + j * LANES, LANES)
                term = table[at_rows, at].astype(F32) * by_row
                acc8[:, at] += jnp.sum(term.reshape(BLOCK // 8, 8, LANES), axis=0)

    def row_exchange_start(sweep):
        for _, k, xx, yy, cc in group:
            pltpu.make_async_remote_copy(
                src_ref=rmsg[sweep],
                dst_ref=rbuf[sweep].at[k - 1],
                send_sem=row_send.at[sweep],
                recv_sem=row_recv.at[sweep],
                device_id=place(xx, z, yy, cc),
                device_id_type=MESH,
            ).start()

    def row_exchange_end(sweep):
        bulk_wait(rbuf[sweep], row_recv.at[sweep])
        return rmsg[sweep][...] + jnp.sum(rbuf[sweep][...], axis=0)

    def scale_probs():
        @pl.loop(0, blocks)
        def _(b):
            at_rows = pl.ds(pl.multiple_of(b * BLOCK, BLOCK), BLOCK)
            by_row = sscale[at_rows, :]
            for j in range(cols // LANES):
                at = pl.ds(j * LANES, LANES)
                expo[at_rows, at] = expo[at_rows, at] * by_row

    for sweep in range(SWEEPS):
        if sweep > 0:
            for q in range(PARTS):
                col_pass(q)
                col_send_part(sweep, q)
        if sweep == 1:
            student_arrived(x_order[-1])
            rmsg[sweep][sz.packed:, :] = pack(sacc)
        for q in range(PARTS):
            col_recv_part(sweep, q)
            row_pass(q)
        rmsg[sweep][0:sz.packed, :] = pack(racc)
        row_exchange_start(sweep)
        if sweep == 0:
            student_forward()
            for d in x_order[:-1]:
                student_arrived(d)
        if sweep == SWEEPS - 1:
            scale_probs()
        total = row_exchange_end(sweep)
        if sweep == 1:
            unpack((LOSS_SCALE / STUDENT_TEMP) / total[sz.packed:, :], sscale)
            total = total[0:sz.packed, :]
        if sweep == SWEEPS - 1:
            unpack((LOSS_SCALE / STUDENT_TEMP) / total, rscale)
        else:
            unpack(1.0 / total, rscale)

    def gradient_tile(t):
        at = pl.ds(t * tile, tile)

        @pl.loop(0, blocks)
        def _(b):
            at_rows = pl.ds(pl.multiple_of(b * BLOCK, BLOCK), BLOCK)
            by_row = rscale[at_rows, :]
            for j in range(chunks):
                at_j = pl.ds(t * tile + j * LANES, LANES)
                target = (table[at_rows, at_j].astype(F32) * by_row) * colv[:, at_j]
                table[at_rows, at_j] = (expo[at_rows, at_j] - target).astype(BF16)

        pg = jnp.dot(sht[...], table[:, at], preferred_element_type=F32)
        inv = winv[:, at]
        pu = wbuf[:, at].astype(F32) * inv
        dots = jnp.sum(pu * pg, axis=0, keepdims=True)
        out = (pg - pu * dots) * inv
        grad[:, :, :, at] = out.reshape(nx, nz, sz.bw, tile)

    def unit_tile(t):
        at = pl.ds(t * tile, tile)
        more = jnp.dot(table[:, at], pht[at, :], preferred_element_type=F32)
        unit[...] = more if t == 0 else unit[...] + more

    def ring_block(stream, s):
        if stream % 2 == 0:
            return (z + 2 * nz - 1 - s) % nz
        return (z + 1 + s) % nz

    def ring_send_copy(stream, s, src):
        return pltpu.make_async_remote_copy(
            src_ref=src,
            dst_ref=ring.at[stream, s],
            send_sem=ring_send.at[stream, s],
            recv_sem=ring_recv.at[stream, s],
            device_id=place(x, zs[1 if stream % 2 == 0 else nz - 1], y, c),
            device_id_type=MESH,
        )

    def begin(stream):
        block = grad.at[:, ring_block(stream, 0), :, pl.ds(stream * tile, tile)]
        ring_send_copy(stream, 0, block).start()

    def serve(stream, s, last=False):
        slot = ring.at[stream, s]
        bulk_wait(slot, ring_recv.at[stream, s])
        at = pl.ds(stream * tile, tile)
        slot[...] = slot[...] + grad[:, ring_block(stream, s + 1), :, at]
        if not last:
            ring_send_copy(stream, s + 1, slot).start()

    def out_slice(stream):
        return gw_ref.at[:, pl.ds(pl.multiple_of(x * cols + stream * tile, tile), tile)]

    def own_copy(stream):
        return pltpu.make_async_copy(
            ring.at[stream, sz.steps - 1, x], out_slice(stream), own_sem.at[stream]
        )

    def deliver(stream):
        for d in reversed(x_order):
            pltpu.make_async_remote_copy(
                src_ref=ring.at[stream, sz.steps - 1, xs[d]],
                dst_ref=out_slice(stream),
                send_sem=x_send.at[stream, d - 1],
                recv_sem=x_recv.at[stream, d - 1],
                device_id=place(xs[d], z, y, c),
                device_id_type=MESH,
            ).start()
        own_copy(stream).start()

    early = range(0, TILES // 2)
    late = range(TILES // 2, TILES)
    for t in range(TILES):
        gradient_tile(t)
        begin(t)
        if t >= len(early) - 1:
            n = t + 1 - len(early)
            serve(n % len(early), n // len(early))
    after = [(late[0], 0)]
    for stream in early[1:]:
        after += [(stream, 1), (len(early) + stream, 0)]
    for t in range(TILES):
        unit_tile(t)
        if t < len(after):
            serve(*after[t])

    def unit_send(entry):
        _, k, xx, yy, cc = entry
        first = xx * rows + (yy * nc + cc) * sz.share
        pltpu.make_async_remote_copy(
            src_ref=unit.at[pl.ds(pl.multiple_of(first, sz.share), sz.share)],
            dst_ref=ubuf.at[k - 1],
            send_sem=u_send,
            recv_sem=u_recv,
            device_id=place(xx, z, yy, cc),
            device_id_type=MESH,
        ).start()

    def ring_steps(first, last):
        @pl.loop(first, last)
        def _(s):
            for stream in late:
                serve(stream, s)
            for stream in early:
                serve(stream, s + 1)

    spaced = max(min(3, sz.steps - 2), 1)
    waiting = list(group)
    slots = (spaced - 1) * TILES
    for n in range(slots):
        s, i = 1 + n // TILES, n % TILES
        if i < len(late):
            serve(late[i], s)
        else:
            serve(early[i - len(late)], s + 1)
        for _ in range(-(-len(group) // slots)):
            if waiting:
                unit_send(waiting.pop(0))
    for entry in waiting:
        unit_send(entry)

    middle = max(sz.steps - 3, spaced)
    ring_steps(spaced, middle)

    mine = pl.ds(pl.multiple_of((y * nc + c) * sz.share, sz.share), sz.share)
    bulk_wait(ubuf, u_recv)
    first = pl.multiple_of(x * rows + (y * nc + c) * sz.share, sz.share)
    total = unit[pl.ds(first, sz.share), :]
    for k in range(sz.group - 1):
        total = total + ubuf[k]
    unit_mine = sbuf[x, mine]
    along = jnp.sum(unit_mine * total, axis=1, keepdims=True)
    rowg[mine, :] = (total - unit_mine * along) / snorm[mine, 0:1]
    for k in range(1, ny * nc):
        pltpu.make_async_remote_copy(
            src_ref=rowg.at[mine],
            dst_ref=rowg.at[mine],
            send_sem=g_send,
            recv_sem=g_recv,
            device_id=place(x, z, ys[k // nc], cs[k % nc]),
            device_id_type=MESH,
        ).start()

    ring_steps(middle, sz.steps - 2)
    for stream in late:
        serve(stream, sz.steps - 2)
    for stream in early:
        serve(stream, sz.steps - 1, last=True)
        deliver(stream)
    for stream in late:
        serve(stream, sz.steps - 1, last=True)
        deliver(stream)

    others = pl.ds(0, rows - sz.share)
    bulk_wait(rowg.at[others], g_recv)
    bulk_wait(rowg.at[others], g_send)
    for which, buf in ((0, tbuf), (1, sbuf)):
        for d in x_order:
            if which == 1 or d in near:
                spread(buf, which, d).wait_send()
            forward(buf, which, d).wait_send()
    if far:
        relay(0).wait_send()
        relay(1).wait_send()
    for sweep in range(SWEEPS):
        for q in range(PARTS):
            bulk_wait(colbuf.at[sweep, q], col_send.at[sweep, q])
        bulk_wait(rbuf[sweep], row_send.at[sweep])
    bulk_wait(ubuf, u_send)

    @pl.loop(0, sz.steps)
    def _(s):
        for stream in range(TILES):
            bulk_wait(ring.at[stream, s], ring_send.at[stream, s])

    for stream in range(TILES):
        own_copy(stream).wait()
        for d in range(1, nx):
            bulk_wait(ring.at[stream, 0, 0], x_send.at[stream, d - 1])
            bulk_wait(ring.at[stream, 0, 0], x_recv.at[stream, d - 1])


def finish(sz, mask_ref, rowg_ref, gw_in, gs_ref, gw_out):
    gw_out[...] = gw_in[...]
    at = lax.broadcasted_iota(jnp.int32, (sz.patches, sz.rows), 0)
    picks = jnp.where(at == mask_ref[...], 1.0, 0.0).astype(BF16)
    rest = rowg_ref[...]
    out = None
    for _ in range(3):
        piece = rest.astype(BF16)
        rest = rest - piece.astype(F32)
        term = jnp.dot(picks, piece, preferred_element_type=F32)
        out = term if out is None else out + term
    gs_ref[...] = out


def per_device(sz, student_patches, teacher_patches, weights_raw, masked_rows):
    vmem = pl.BlockSpec(memory_space=pltpu.VMEM)
    anywhere = pl.BlockSpec(memory_space=pl.ANY)
    dma = pltpu.SemaphoreType.DMA
    g = sz.group
    nx, nz = sz.nx, sz.nz
    p = sz.packed
    scratch = [
        pltpu.VMEM((sz.patches, sz.width), BF16),
        pltpu.VMEM((sz.patches, sz.width), BF16),
        pltpu.VMEM((sz.width, sz.cols), BF16),
        pltpu.VMEM((sz.width, sz.cols), BF16),
        pltpu.VMEM((sz.cols, sz.width), BF16),
        pltpu.VMEM((1, sz.cols), F32),
        pltpu.VMEM((nx, sz.rows, sz.width), F32),
        pltpu.VMEM((nx, sz.rows, sz.width), F32),
        pltpu.VMEM((sz.rows, LANES), F32),
        pltpu.VMEM((sz.width, sz.all_rows), BF16),
        pltpu.VMEM((sz.all_rows, sz.cols), BF16),
        pltpu.VMEM((sz.all_rows, sz.cols), F32),
        pltpu.VMEM((8, sz.cols), F32),
        pltpu.VMEM((1, sz.cols), F32),
        pltpu.VMEM((SWEEPS, PARTS, 1, sz.part), F32),
        pltpu.VMEM((SWEEPS, PARTS, nz - 1, 1, sz.part), F32),
        pltpu.VMEM((sz.all_rows, LANES), F32),
        pltpu.VMEM((sz.all_rows, LANES), F32),
        pltpu.VMEM((sz.all_rows, LANES), F32),
        pltpu.VMEM((sz.all_rows, LANES), F32),
        pltpu.VMEM((p, LANES), F32),
        pltpu.VMEM((2 * p, LANES), F32),
        pltpu.VMEM((p, LANES), F32),
        pltpu.VMEM((g - 1, p, LANES), F32),
        pltpu.VMEM((g - 1, 2 * p, LANES), F32),
        pltpu.VMEM((g - 1, p, LANES), F32),
        pltpu.VMEM((sz.all_rows, sz.width), F32),
        pltpu.VMEM((g - 1, sz.share, sz.width), F32),
        pltpu.VMEM((nx, nz, sz.bw, sz.cols), F32),
        pltpu.VMEM((TILES, sz.steps, nx, sz.bw, sz.tile), F32),
        dma((2,)),
        dma(()),
        dma((TILES,)),
        dma((2, nx - 1)),
        dma((2, nx - 1)),
        dma((2,)),
        dma((2,)),
        dma((2, nx - 1)),
        dma((2, nx - 1)),
        dma((SWEEPS, PARTS)),
        dma((SWEEPS, PARTS)),
        dma((SWEEPS,)),
        dma((SWEEPS,)),
        dma(()),
        dma(()),
        dma(()),
        dma(()),
        dma((TILES, sz.steps)),
        dma((TILES, sz.steps)),
        dma((TILES, nx - 1)),
        dma((TILES, nx - 1)),
    ]
    picked = masked_rows.reshape(1, sz.rows)
    row_grad, grad_weight = pl.pallas_call(
        functools.partial(kernel, sz),
        out_shape=(
            jax.ShapeDtypeStruct((sz.rows, sz.width), F32),
            jax.ShapeDtypeStruct((sz.bw, sz.cols_dp), F32),
        ),
        in_specs=[vmem, anywhere, anywhere, anywhere],
        out_specs=(vmem, anywhere),
        scratch_shapes=scratch,
        compiler_params=pltpu.CompilerParams(
            collective_id=0, has_side_effects=True, vmem_limit_bytes=56 * 1024 * 1024
        ),
        cost_estimate=pl.CostEstimate(
            flops=8 * sz.all_rows * sz.cols * sz.width,
            bytes_accessed=4 * sz.width * sz.cols,
            transcendentals=2 * sz.all_rows * sz.cols,
        ),
        name="sinkhorn_loss",
    )(picked, student_patches, teacher_patches, weights_raw)
    return pl.pallas_call(
        functools.partial(finish, sz),
        out_shape=(
            jax.ShapeDtypeStruct((sz.patches, sz.width), F32),
            jax.ShapeDtypeStruct((sz.bw, sz.cols_dp), F32),
        ),
        in_specs=[vmem, vmem, vmem],
        out_specs=(vmem, vmem),
        name="finish",
    )(picked, row_grad, grad_weight)


def solution(mesh):
    placed = (P("dp", None), P("dp", None), P(None, "proto"), P("dp"))
    mesh_shape = (mesh.shape["dp"], mesh.shape["proto"])

    def body(student_patches, teacher_patches, weights_raw, masked_rows):
        sz = Sizes(
            mesh_shape,
            weights_raw.shape[0],
            student_patches.shape[0],
            masked_rows.shape[0],
            weights_raw.shape[1],
        )
        return per_device(sz, student_patches, teacher_patches, weights_raw, masked_rows)

    return jax.shard_map(
        body,
        mesh=mesh,
        in_specs=placed,
        out_specs=(P("dp", None), P("dp", "proto")),
        check_vma=False,
    )
```
